128 devices in a mesh: ha: 16 (over x_hi, z, core), wa: 8 (over y, x_lo).
Axes of the slice: x: 4 (x_hi: 2, x_lo: 2; x = x_hi * 2 + x_lo), y: 4, z: 4, core: 2. Of those that a mesh axis runs over, the one named last changes fastest.
Arguments:
- latents: bfloat16 [2, 256, 128, 3072], P(None, 'ha', 'wa'), may hold values from -70 to 70
- cond_mask: int32 [2, 256, 128], P(None, 'ha', 'wa'), may hold values 0 or 1
- radii: int32 [12, 2], replicated, may hold values from 0 to 1, as said below
- cond_embed: float32 [3072], replicated, may hold values from -6 to 6
- mod_shift: float32 [3072], replicated, may hold values from -3 to 3
- mod_scale: float32 [3072], replicated, may hold values from -3 to 3
- w_qkv: bfloat16 [3072, 4608], P(('ha', 'wa')), as said below
- q_gain: float32 [128], replicated, may hold values from 0.5 to 6
- k_gain: float32 [128], replicated, may hold values from 0.5 to 6
Outputs:
- attended: bfloat16 [2, 256, 128, 1536], P(None, 'ha', 'wa')
The draws below stay inside these ranges and needn't reach their ends.
Inputs may be any that keep to these rules, and one draw needn't show every extreme that they name: `radii`: some head has radius 1 along both rows and columns, some head has radius 0 along rows. `w_qkv`: entries lie within 5 / sqrt(3072) in magnitude.
All inputs are finite; a program needn't handle non-finite values. No bound on the sum of `cond_mask` on one device may be relied on, other than what follows from the above.
Results may differ from the reference program's by a relative error of at most 0.0056.
Values may be sent and summed in bfloat16 or wider, within the bound.
No kernel may reach another device: no remote copies, remote signals or barrier semaphores. Data moves between devices by JAX's collectives and lax.ppermute only.
A program may use at most 192 MiB of HBM per device.

```python
import math
import jax
import jax.numpy as jnp
from jax import lax

D = 3072
HEADS = 12
HD = 128
TILE = 8
FR = 2
H = 256
W = 128


def draw_latents(key, part):
    key = jax.random.fold_in(key, 3)
    first = jax.random.fold_in(key, 0)
    shape = (FR, H, W, D)
    base = jnp.clip(jax.random.normal(first, shape, jnp.float32), -6.0, 6.0)
    return base.astype(jnp.bfloat16)


def draw_radii(key, part):
    key = jax.random.fold_in(key, 11)
    first, second, third = jax.random.split(key, 3)
    values = (jax.random.randint(first, (HEADS, 2), 0, 4) > 0).astype(jnp.int32)
    chosen = jax.random.randint(second, (), 0, HEADS)
    other = (chosen + 1 + jax.random.randint(third, (), 0, HEADS - 1)) % HEADS
    head_ids = jnp.arange(HEADS)[:, None]
    axis_ids = jnp.arange(2)[None, :]
    values = jnp.where(head_ids == chosen, 1, values)
    values = jnp.where((head_ids == other) & (axis_ids == 0), 0, values)
    return values.astype(jnp.int32)


def draw_w_qkv(key, part):
    key = jax.random.fold_in(key, 5)
    first = jax.random.fold_in(key, 0)
    shape = (D, 3, HEADS, HD)
    base = jnp.clip(jax.random.normal(first, shape, jnp.float32), -5.0, 5.0) / math.sqrt(D)
    return base.reshape(D, 3 * HEADS * HD).astype(jnp.bfloat16)


def gain_values(key):
    return jnp.exp(jax.random.uniform(key, (HD,), jnp.float32, math.log(0.5), math.log(2.0)))


def draw_q_gain(key, part):
    key = jax.random.fold_in(key, 7)
    return gain_values(key)


def draw_k_gain(key, part):
    key = jax.random.fold_in(key, 9)
    return gain_values(key)


def with_ends(entries, own_key, low, high):
    shape = entries.shape
    place = [jax.random.randint(jax.random.fold_in(own_key, axis), (), 0, shape[axis]) for axis in range(len(shape))]
    entries = entries.at[tuple(place)].set(low)
    longest = shape.index(max(shape))
    place[longest] = (place[longest] + 1) % shape[longest]
    return entries.at[tuple(place)].set(high)


def centred(own_key, extent, deviation, bound, held_as=jnp.bfloat16):
    array = deviation * jax.random.normal(own_key, extent, jnp.float32)
    return jnp.clip(array, min=-bound, max=bound).astype(held_as)


def setup_inputs(seed: int = 0) -> dict:
    key_list = jax.random.split(jax.random.key(seed), 10)
    return {
        "latents": draw_latents(jax.random.fold_in(key_list[9], 71), 0),
        "cond_mask": with_ends((jax.random.randint(key_list[1], (FR, H, W), 0, 2) < 1).astype(jnp.int32), jax.random.fold_in(key_list[1], 1), 0, 1),
        "radii": draw_radii(jax.random.fold_in(key_list[9], 71), 0),
        "cond_embed": centred(key_list[3], (D,), 1.0, 6.0, jnp.float32),
        "mod_shift": centred(key_list[4], (D,), 0.5, 3.0, jnp.float32),
        "mod_scale": centred(key_list[5], (D,), 0.5, 3.0, jnp.float32),
        "w_qkv": draw_w_qkv(jax.random.fold_in(key_list[9], 71), 0),
        "q_gain": draw_q_gain(jax.random.fold_in(key_list[9], 71), 0),
        "k_gain": draw_k_gain(jax.random.fold_in(key_list[9], 71), 0),
    }


def normalize(latents, cond_mask, cond_embed, mod_shift, mod_scale):
    cond = latents.astype(jnp.float32) + cond_mask[..., None].astype(jnp.float32) * cond_embed
    center = cond - lax.optimization_barrier(jnp.mean(cond, axis=-1, keepdims=True))
    spread = lax.optimization_barrier(jnp.mean(center * center, axis=-1, keepdims=True))
    return (center * lax.rsqrt(spread + 1e-06) * (1.0 + mod_scale) + mod_shift).astype(jnp.bfloat16)

def head_norm(block, gain):
    square = lax.optimization_barrier(jnp.mean(block * block, axis=-1, keepdims=True))
    return (block * lax.rsqrt(square + 1e-06) * gain).astype(jnp.bfloat16)

def split_heads(qkv, heads, size, q_gain, k_gain):
    parts = qkv.reshape(qkv.shape[0], 3, heads, size)
    return (head_norm(parts[:, 0], q_gain), head_norm(parts[:, 1], k_gain), parts[:, 2].astype(jnp.bfloat16))

def reference(latents, cond_mask, radii, cond_embed, mod_shift, mod_scale, w_qkv, q_gain, k_gain):
    frames, rows, cols, width = latents.shape
    heads = radii.shape[0]
    size = q_gain.shape[0]
    blocks = rows // TILE
    across = cols // TILE
    scale = 1.0 / math.sqrt(size)
    stacked = latents.reshape(frames, blocks, TILE, cols, width).transpose(1, 0, 2, 3, 4)
    marks = cond_mask.reshape(frames, blocks, TILE, cols).transpose(1, 0, 2, 3)

    def project(item):
        block, mark = item
        normed = normalize(block, mark, cond_embed, mod_shift, mod_scale).reshape(-1, width)
        qkv = jnp.dot(normed, w_qkv, preferred_element_type=jnp.float32)
        query, key, value = split_heads(qkv, heads, size, q_gain, k_gain)
        shape = (frames, TILE, cols, heads, size)
        return (query.reshape(shape), key.reshape(shape), value.reshape(shape))
    query, key, value = lax.map(project, (stacked, marks))

    def unstack(part):
        return part.transpose(1, 0, 2, 3, 4, 5).reshape(frames, rows, cols, heads, size)
    query, key, value = (unstack(query), unstack(key), unstack(value))
    padding = ((0, 0), (TILE, TILE), (TILE, TILE), (0, 0), (0, 0))
    key_pad = jnp.pad(key, padding)
    value_pad = jnp.pad(value, padding)
    row_pos = jnp.arange(rows + 2 * TILE, dtype=jnp.int32) - TILE
    col_pos = jnp.arange(cols + 2 * TILE, dtype=jnp.int32) - TILE
    row_ok = (row_pos >= 0) & (row_pos < rows)
    col_ok = (col_pos >= 0) & (col_pos < cols)
    span = 3 * TILE
    offset = jnp.abs(jnp.arange(span, dtype=jnp.int32) // TILE - 1)
    dist_h = jnp.broadcast_to(offset[:, None], (frames, span, span)).reshape(-1)
    dist_w = jnp.broadcast_to(offset[None, :], (frames, span, span)).reshape(-1)
    zero = jnp.zeros((), jnp.int32)

    def attend(index):
        tile_r = (index // across).astype(jnp.int32)
        tile_c = (index % across).astype(jnp.int32)
        r0 = (tile_r * TILE).astype(jnp.int32)
        c0 = (tile_c * TILE).astype(jnp.int32)
        q_tile = lax.dynamic_slice(query, (zero, r0, c0, zero, zero), (frames, TILE, TILE, heads, size)).reshape(-1, heads, size)
        k_tile = lax.dynamic_slice(key_pad, (zero, r0, c0, zero, zero), (frames, span, span, heads, size)).reshape(-1, heads, size)
        v_tile = lax.dynamic_slice(value_pad, (zero, r0, c0, zero, zero), (frames, span, span, heads, size)).reshape(-1, heads, size)
        row_valid = lax.dynamic_slice(row_ok, (r0,), (span,))
        col_valid = lax.dynamic_slice(col_ok, (c0,), (span,))
        valid = jnp.broadcast_to(row_valid[:, None] & col_valid[None, :], (frames, span, span)).reshape(-1)
        allowed = valid[None, :] & (dist_h[None, :] <= radii[:, 0:1]) & (dist_w[None, :] <= radii[:, 1:2])
        score = jnp.einsum('qhd,khd->hqk', q_tile.astype(jnp.float32), k_tile.astype(jnp.float32)) * scale
        score = jnp.where(allowed[:, None, :], score, -1e+30)
        top = lax.optimization_barrier(jnp.max(score, axis=-1, keepdims=True))
        prob = jnp.exp(score - top)
        total = lax.optimization_barrier(jnp.sum(prob, axis=-1))
        weights = prob.astype(jnp.bfloat16)
        mixed = jnp.einsum('hqk,khd->qhd', weights.astype(jnp.float32), v_tile.astype(jnp.float32))
        mixed = mixed / total.T[:, :, None]
        return mixed.astype(jnp.bfloat16).reshape(frames, TILE, TILE, heads * size)
    tiles = lax.map(attend, jnp.arange(blocks * across, dtype=jnp.int32))
    tiles = tiles.reshape(blocks, across, frames, TILE, TILE, heads * size)
    return tiles.transpose(2, 0, 3, 1, 4, 5).reshape(frames, rows, cols, heads * size)
```

```python
import math

import jax
import jax.numpy as jnp
from jax import lax
from jax.experimental import pallas as pl
from jax.experimental.pallas import tpu as pltpu
from jax.sharding import PartitionSpec as P

AXES = ("ha", "wa")
NX_HI, NZ, NY, NX_LO = 2, 4, 4, 2
ROWS_OF_CHIPS, COLS_OF_CHIPS = NX_HI * NZ, NY * NX_LO
F32, BF16 = jnp.float32, jnp.bfloat16
D, HD, TOK = 3072, 128, 128
HALF_HEADS, PART_HEADS = 6, 3
PART = PART_HEADS * HD
MIB = 1024 * 1024


def index_of(x_hi, z, core, y, x_lo):
    return ((x_hi * NZ + z) * 2 + core) * COLS_OF_CHIPS + y * NX_LO + x_lo


def permutation(move):
    pairs = []
    for x_hi in range(NX_HI):
        for z in range(NZ):
            for core in range(2):
                for y in range(NY):
                    for x_lo in range(NX_LO):
                        target = move(x_hi, z, core, y, x_lo)
                        if target is not None:
                            pairs.append((index_of(x_hi, z, core, y, x_lo), index_of(*target)))
    return pairs


def swap_core(x_hi, z, core, y, x_lo):
    return x_hi, z, 1 - core, y, x_lo


def flip_x(bits):
    return lambda x_hi, z, core, y, x_lo: (x_hi ^ (bits >> 1), z, core, y, x_lo ^ (bits & 1))


def step_y(by):
    return lambda x_hi, z, core, y, x_lo: (x_hi, z, core, (y + by) % NY, x_lo)


def step_z(by):
    return lambda x_hi, z, core, y, x_lo: (x_hi, (z + by) % NZ, core, y, x_lo)


def next_col(by):
    def move(x_hi, z, core, y, x_lo):
        wa = y * NX_LO + x_lo + by
        if not 0 <= wa < COLS_OF_CHIPS:
            return None
        return x_hi, z, core, wa // NX_LO, wa % NX_LO

    return move


def next_row(by):
    def move(x_hi, z, core, y, x_lo):
        q = x_hi * NZ + z + by
        if not 0 <= q < ROWS_OF_CHIPS:
            return None
        return q // NZ, q % NZ, core, y, x_lo

    return move


def send(array, move):
    return lax.ppermute(array, AXES, permutation(move))


def norm_kernel(lat_ref, mask_ref, embed_ref, shift_ref, scale_ref, left_ref, right_ref):
    cond = lat_ref[0].astype(F32) + mask_ref[0] * embed_ref[...]
    center = cond - jnp.mean(cond, axis=-1, keepdims=True)
    spread = jnp.mean(center * center, axis=-1, keepdims=True)
    normed = center * lax.rsqrt(spread + 1e-06) * (1.0 + scale_ref[...]) + shift_ref[...]
    left_ref[0, 0] = normed[:, :8].reshape(64, D).astype(BF16)
    right_ref[0, 0] = normed[:, 8:].reshape(64, D).astype(BF16)


def normalize(latents, cond_mask, cond_embed, mod_shift, mod_scale):
    vector = pl.BlockSpec((1, 1, D), lambda t, f: (0, 0, 0))
    tile = pl.BlockSpec((1, 1, 64, D), lambda t, f: (t, f, 0, 0))
    shape = jax.ShapeDtypeStruct((2, 2, 64, D), BF16)
    left, right = pl.pallas_call(
        norm_kernel,
        grid=(2, 2),
        in_specs=[
            pl.BlockSpec((1, 8, 16, D), lambda t, f: (f, t, 0, 0)),
            pl.BlockSpec((1, 8, 16, 1), lambda t, f: (f, t, 0, 0)),
            vector,
            vector,
            vector,
        ],
        out_specs=[tile, tile],
        out_shape=[shape, shape],
        compiler_params=pltpu.CompilerParams(vmem_limit_bytes=48 * MIB),
        name="norm",
    )(
        latents,
        cond_mask.astype(F32)[..., None],
        cond_embed.reshape(1, 1, D),
        mod_shift.reshape(1, 1, D),
        mod_scale.reshape(1, 1, D),
    )
    return left.reshape(2, TOK, D), right.reshape(2, TOK, D)


def ring(chunk, step):
    half = chunk.shape[0] // 2
    before = send(chunk, step(1))
    after = send(chunk, step(-1))
    low = send(before[:half], step(1))
    high = send(after[half:], step(-1))
    return chunk, before, after, low, high


def joined(pieces):
    own, before, after, low, high = pieces
    return jnp.stack([own, after, jnp.concatenate([low, high]), before])


def gather_weights(w_qkv, core, x_lo, x_hi):
    rows = w_qkv.shape[0]
    split = w_qkv.reshape(rows, 3, 2, 2, PART)
    first, second = split[:, :, 0], split[:, :, 1]
    mine = jnp.where(core == 0, first, second)
    theirs = jnp.where(core == 0, second, first)
    got = send(theirs, swap_core)
    both = jnp.where(core == 0, jnp.stack([mine, got]), jnp.stack([got, mine]))
    flips = [both] + [send(both, flip_x(bits)) for bits in (1, 2, 3)]

    def pair(same, other):
        return jnp.where(
            x_lo == 0,
            jnp.concatenate([same, other], axis=1),
            jnp.concatenate([other, same], axis=1),
        )

    here, there = pair(flips[0], flips[1]), pair(flips[2], flips[3])
    block = jnp.where(x_hi == 0, jnp.stack([here, there]), jnp.stack([there, here]))
    parts = [
        block[:, :, :, :, p].reshape(2, 2, 2 * rows, 3 * PART) for p in range(2)
    ]
    along_y, along_z = ring(parts[0], step_y), ring(parts[1], step_z)
    return ring(joined(along_y), step_z), ring(joined(along_z), step_y)


def exchange_rows(own, other, core):
    down = jnp.where(core == 0, other[0][1], own[1][1])
    up = jnp.where(core == 0, own[0][0], other[1][0])
    above, below = send(down, next_row(1)), send(up, next_row(-1))
    return above, below, send(above, swap_core), send(below, swap_core)


def attend_kernel(place_ref, radii_ref, q_gain_ref, k_gain_ref, *refs):
    (own_l, own_r, oth_l, oth_r, far_l, far_r, oth_far_l, oth_far_r) = refs[:8]
    near_rows, corner_rows = refs[8:12], refs[12:16]
    pieces = (refs[16:21], refs[21:26])
    out_ref = refs[26]
    xs, ws, qs, ks, vs, x_sem, w_sem = refs[27:]
    core, row, col, z, y = (place_ref[i] for i in range(5))

    for p in range(2):
        mine, before, after, low, high = pieces[p]
        other_at, ring_at = (y, z) if p == 0 else (z, y)
        for n in range(4):
            sources = (
                (mine.at[n], 0),
                (after.at[n], 1),
                ((low if n < 2 else high).at[n % 2], 2),
                (before.at[n], 3),
            )
            inner = lax.rem(other_at + n, 4)
            for source, by in sources:
                outer = lax.rem(ring_at + by, 4)
                at_z, at_y = (outer, inner) if p == 0 else (inner, outer)
                pltpu.make_async_copy(
                    source, ws.at[p, :, at_z, :, at_y], w_sem.at[p, n, by]
                ).start()

    def fetch(source, tile_row, tile_col):
        at = tile_row * 4 + tile_col
        pltpu.make_async_copy(source, xs.at[at], x_sem.at[at]).start()

    fetch(near_rows[0], 0, 1 + core)
    fetch(near_rows[2], 0, 2 - core)
    fetch(corner_rows[0], 0, 3 * core)
    fetch(corner_rows[2], 0, 3 - 3 * core)
    for i in range(2):
        first, second = 1 + 2 * core + i, 3 - 2 * core + i
        for c, source in enumerate((far_l, own_l, own_r, far_r)):
            fetch(source.at[i], first, c)
        for c, source in enumerate((oth_far_l, oth_l, oth_r, oth_far_r)):
            fetch(source.at[i], second, c)
    fetch(near_rows[1], 5, 1 + core)
    fetch(near_rows[3], 5, 2 - core)
    fetch(corner_rows[1], 5, 3 * core)
    fetch(corner_rows[3], 5, 3 - 3 * core)

    for p in range(2):
        for n in range(4):
            for by in range(4):
                pltpu.make_async_copy(
                    ws.at[p, :, by, :, n], ws.at[p, :, by, :, n], w_sem.at[p, n, by]
                ).wait()

    def head_norm(block, gain_ref):
        square = jnp.mean(block * block, axis=-1, keepdims=True)
        return (block * lax.rsqrt(square + 1e-06) * gain_ref[...]).astype(BF16)

    def project(r, _):
        for c in range(4):
            at = r * 4 + c
            pltpu.make_async_copy(xs.at[at], xs.at[at], x_sem.at[at]).wait()
        for p in range(2):
            x = xs[pl.ds(r * 4, 4)].reshape(4 * TOK, D)
            keyval = jnp.dot(
                x, ws[p, :, :, :, :, :, PART:].reshape(D, 2 * PART), preferred_element_type=F32
            )
            for h in range(PART_HEADS):
                head = p * PART_HEADS + h
                key = head_norm(keyval[:, h * HD : (h + 1) * HD], k_gain_ref)
                ks[head, pl.ds(r * 4, 4)] = key.reshape(4, TOK, HD)
                value = keyval[:, PART + h * HD : PART + (h + 1) * HD].astype(BF16)
                vs[head, pl.ds(r * 4, 4)] = value.reshape(4, TOK, HD)

            @pl.when((r >= 1) & (r <= 4))
            def _():
                x = xs[pl.ds(r * 4 + 1, 2)].reshape(2 * TOK, D)
                query = jnp.dot(
                    x, ws[p, :, :, :, :, :, :PART].reshape(D, PART), preferred_element_type=F32
                )
                for h in range(PART_HEADS):
                    block = head_norm(query[:, h * HD : (h + 1) * HD], q_gain_ref)
                    qs[p * PART_HEADS + h, pl.ds((r - 1) * 2, 2)] = block.reshape(2, TOK, HD)

        return 0

    lax.fori_loop(0, 6, project, 0)

    factor = math.log2(math.e) / math.sqrt(HD)

    def attend(s, _):
        tile = jnp.where(s < 4, 4 * (1 - core) + s, 4 * core + s - 4)
        r, c = 1 + tile // 2, 1 + tile % 2
        for h in range(HALF_HEADS):
            reach_r, reach_c = radii_ref[core * HALF_HEADS + h, 0], radii_ref[core * HALF_HEADS + h, 1]
            q = qs[h, tile]
            scores, hidden = [], []
            top = None
            for dr in (-1, 0, 1):
                at = (r + dr) * 4 + c - 1
                k = ks[h, pl.ds(at, 3)].reshape(3 * TOK, HD)
                score = lax.dot_general(
                    q, k, (((1,), (1,)), ((), ())), preferred_element_type=F32
                )
                for dc in (-1, 0, 1):
                    block = score[:, (dc + 1) * TOK : (dc + 2) * TOK]
                    tile_r, tile_c = row * 4 + r - 1 + dr, col * 2 + c - 1 + dc
                    seen = (
                        (abs(dr) <= reach_r)
                        & (abs(dc) <= reach_c)
                        & (tile_r >= 0)
                        & (tile_r < 4 * ROWS_OF_CHIPS)
                        & (tile_c >= 0)
                        & (tile_c < 2 * COLS_OF_CHIPS)
                    )
                    offset = jnp.where(seen, 0.0, 1e30).astype(F32)
                    scores.append(block)
                    hidden.append(offset)
                    shown = block - offset
                    top = shown if top is None else jnp.maximum(top, shown)
            peak = jnp.max(top, axis=-1, keepdims=True) * factor
            total = None
            mixed = None
            for j, dr in enumerate((-1, 0, 1)):
                weights = []
                for i in range(3):
                    n = 3 * j + i
                    prob = jnp.exp2(scores[n] * factor - (peak + hidden[n]))
                    total = prob if total is None else total + prob
                    weights.append(prob.astype(BF16))
                at = (r + dr) * 4 + c - 1
                v = vs[h, pl.ds(at, 3)].reshape(3 * TOK, HD)
                term = jnp.dot(
                    jnp.concatenate(weights, axis=1), v, preferred_element_type=F32
                )
                mixed = term if mixed is None else mixed + term
            den = jnp.sum(total, axis=-1, keepdims=True)
            out_ref[s, :, h * HD : (h + 1) * HD] = (mixed / den).astype(BF16)
        return 0

    lax.fori_loop(0, 8, attend, 0)


def attend(place, radii, q_gain, k_gain, tokens, pieces):
    smem = pl.BlockSpec(memory_space=pltpu.SMEM)
    vmem = pl.BlockSpec(memory_space=pltpu.VMEM)
    hbm = pl.BlockSpec(memory_space=pl.ANY)
    return pl.pallas_call(
        attend_kernel,
        in_specs=[smem, smem, vmem, vmem] + [hbm] * (len(tokens) + len(pieces)),
        out_specs=vmem,
        out_shape=jax.ShapeDtypeStruct((8, TOK, HALF_HEADS * HD), BF16),
        scratch_shapes=[
            pltpu.VMEM((24, TOK, D), BF16),
            pltpu.VMEM((2, NX_HI, NZ, 2, NY, 48, 3 * PART), BF16),
            pltpu.VMEM((HALF_HEADS, 8, TOK, HD), BF16),
            pltpu.VMEM((HALF_HEADS, 24, TOK, HD), BF16),
            pltpu.VMEM((HALF_HEADS, 24, TOK, HD), BF16),
            pltpu.SemaphoreType.DMA((24,)),
            pltpu.SemaphoreType.DMA((2, 4, 4)),
        ],
        compiler_params=pltpu.CompilerParams(vmem_limit_bytes=60 * MIB),
        cost_estimate=pl.CostEstimate(
            flops=45 * 10**9, bytes_accessed=35 * 10**6, transcendentals=8 * 10**6
        ),
        name="attend",
    )(place, radii, q_gain.reshape(1, HD), k_gain.reshape(1, HD), *tokens, *pieces)


def assemble_kernel(place_ref, mine_ref, got_ref, out_ref):
    first = place_ref[0] == 0

    def rows(ref):
        halves = [ref[0, c, 0].astype(F32).reshape(8, 8, HALF_HEADS * HD) for c in range(2)]
        return jnp.concatenate(halves, axis=1)

    mine, got = rows(mine_ref), rows(got_ref)
    width = HALF_HEADS * HD
    out_ref[0, :, :, :width] = jnp.where(first, mine, got).astype(BF16)
    out_ref[0, :, :, width:] = jnp.where(first, got, mine).astype(BF16)


def assemble(place, mine, got):
    width = HALF_HEADS * HD
    shape = (2, 2, 2, 64, width)
    tiles = pl.BlockSpec((1, 2, 1, 64, width), lambda t, f: (t, 0, f, 0, 0))
    return pl.pallas_call(
        assemble_kernel,
        grid=(2, 2),
        in_specs=[pl.BlockSpec(memory_space=pltpu.SMEM), tiles, tiles],
        out_specs=pl.BlockSpec((1, 8, 16, 2 * width), lambda t, f: (f, t, 0, 0)),
        out_shape=jax.ShapeDtypeStruct((2, 16, 16, 2 * width), BF16),
        name="assemble",
    )(place, mine.reshape(shape), got.reshape(shape))


def local(latents, cond_mask, radii, cond_embed, mod_shift, mod_scale, w_qkv, q_gain, k_gain):
    ha, wa = lax.axis_index("ha"), lax.axis_index("wa")
    core, row = ha % 2, ha // 2
    x_hi, z, y, x_lo = row // NZ, row % NZ, wa // NX_LO, wa % NX_LO
    place = jnp.stack([core, row, wa, z, y]).astype(jnp.int32)

    part_0, part_1 = gather_weights(w_qkv, core, x_lo, x_hi)

    left, right = normalize(latents, cond_mask, cond_embed, mod_shift, mod_scale)
    oth_left, oth_right = send(left, swap_core), send(right, swap_core)
    near_rows = exchange_rows((left, right), (oth_left, oth_right), core)
    far_left, far_right = send(right, next_col(1)), send(left, next_col(-1))
    oth_far_left, oth_far_right = send(far_left, swap_core), send(far_right, swap_core)
    corner_rows = exchange_rows((far_left, far_right), (oth_far_left, oth_far_right), core)

    tokens = (left, right, oth_left, oth_right, far_left, far_right, oth_far_left, oth_far_right)
    mixed = attend(
        place, radii, q_gain, k_gain, tokens + near_rows + corner_rows, part_0 + part_1
    )
    got = send(mixed[:4], swap_core)
    return assemble(place, mixed[4:], got)


def solution(mesh):
    in_specs = (
        P(None, "ha", "wa", None),
        P(None, "ha", "wa"),
        P(),
        P(),
        P(),
        P(),
        P(("ha", "wa"), None),
        P(),
        P(),
    )
    out_specs = P(None, "ha", "wa", None)
    return jax.shard_map(local, mesh=mesh, in_specs=in_specs, out_specs=out_specs, check_vma=False)
```

```python
import functools
import math

import jax
import jax.numpy as jnp
from jax import lax
from jax.experimental import pallas as pl
from jax.experimental.pallas import tpu as pltpu
from jax.sharding import PartitionSpec as P

AXES = ("ha", "wa")
NX_HI, NZ, NY, NX_LO = 2, 4, 4, 2
ROWS_OF_CHIPS, COLS_OF_CHIPS = NX_HI * NZ, NY * NX_LO
F32, BF16 = jnp.float32, jnp.bfloat16
D, HD, TOK = 3072, 128, 128
HALF_HEADS, PAIRS = 6, 3
PAIR = 2 * HD
MIB = 1024 * 1024


def index_of(x_hi, z, core, y, x_lo):
    return ((x_hi * NZ + z) * 2 + core) * COLS_OF_CHIPS + y * NX_LO + x_lo


def permutation(move):
    pairs = []
    for x_hi in range(NX_HI):
        for z in range(NZ):
            for core in range(2):
                for y in range(NY):
                    for x_lo in range(NX_LO):
                        target = move(x_hi, z, core, y, x_lo)
                        if target is not None:
                            pairs.append((index_of(x_hi, z, core, y, x_lo), index_of(*target)))
    return pairs


def swap_core(x_hi, z, core, y, x_lo):
    return x_hi, z, 1 - core, y, x_lo


def flip_x(bits):
    return lambda x_hi, z, core, y, x_lo: (x_hi ^ (bits >> 1), z, core, y, x_lo ^ (bits & 1))


def swap_beside(x_hi, z, core, y, x_lo):
    return x_hi, z, core, y, 1 - x_lo


def swap_diagonal(x_hi, z, core, y, x_lo):
    wa = y * NX_LO + x_lo + (1 if x_lo else -1)
    if not 0 <= wa < COLS_OF_CHIPS:
        return None
    return x_hi, z, core, wa // NX_LO, wa % NX_LO


def next_row(by):
    def move(x_hi, z, core, y, x_lo):
        q = x_hi * NZ + z + by
        if not 0 <= q < ROWS_OF_CHIPS:
            return None
        return q // NZ, q % NZ, core, y, x_lo

    return move


def send(array, move):
    return lax.ppermute(array, AXES, permutation(move))


def norm_kernel(place_ref, lat_ref, mask_ref, embed_ref, shift_ref, scale_ref, near_ref, far_ref):
    cond = lat_ref[0].astype(F32) + mask_ref[0] * embed_ref[...]
    center = cond - jnp.mean(cond, axis=-1, keepdims=True)
    spread = jnp.mean(center * center, axis=-1, keepdims=True)
    normed = center * lax.rsqrt(spread + 1e-06) * (1.0 + scale_ref[...]) + shift_ref[...]
    left, right = normed[:, :8].reshape(64, D), normed[:, 8:].reshape(64, D)
    first = place_ref[1] == 0
    near_ref[0] = jnp.where(first, right, left).astype(BF16)
    far_ref[0] = jnp.where(first, left, right).astype(BF16)


def normalize(tile_row, x_lo, latents, mask, cond_embed, mod_shift, mod_scale):
    vector = pl.BlockSpec((1, 1, D), lambda f, t: (0, 0, 0))
    tile = pl.BlockSpec((1, 64, D), lambda f, t: (f, 0, 0))
    shape = jax.ShapeDtypeStruct((2, 64, D), BF16)
    left, right = pl.pallas_call(
        norm_kernel,
        grid_spec=pltpu.PrefetchScalarGridSpec(
            num_scalar_prefetch=1,
            grid=(2,),
            in_specs=[
                pl.BlockSpec((1, 8, 16, D), lambda f, t: (f, t[0], 0, 0)),
                pl.BlockSpec((1, 8, 16, 1), lambda f, t: (f, t[0], 0, 0)),
                vector,
                vector,
                vector,
            ],
            out_specs=[tile, tile],
        ),
        out_shape=[shape, shape],
        compiler_params=pltpu.CompilerParams(vmem_limit_bytes=48 * MIB),
        name="norm",
    )(
        jnp.stack([tile_row, x_lo]).astype(jnp.int32),
        latents,
        mask,
        cond_embed.reshape(1, 1, D),
        mod_shift.reshape(1, 1, D),
        mod_scale.reshape(1, 1, D),
    )
    return left.reshape(TOK, D), right.reshape(TOK, D)


def x_block(w_qkv, core, x_lo, x_hi, first_tile):
    rows = w_qkv.shape[0]
    split = w_qkv.reshape(rows, 3, 2, HALF_HEADS * HD)
    first, second = split[:, :, 0], split[:, :, 1]
    mine = jnp.where(core == 0, first, second)
    theirs = jnp.where(core == 0, second, first)
    got = send(theirs, swap_core)
    both = jnp.where(core == 0, jnp.stack([mine, got]), jnp.stack([got, mine]))
    (both,) = held_back((both,), first_tile)
    flips = [both] + [send(both, flip_x(bits)) for bits in (1, 2, 3)]

    def pair(same, other):
        return jnp.where(
            x_lo == 0,
            jnp.concatenate([same, other], axis=1),
            jnp.concatenate([other, same], axis=1),
        )

    here, there = pair(flips[0], flips[1]), pair(flips[2], flips[3])
    return jnp.where(x_hi == 0, jnp.stack([here, there]), jnp.stack([there, here]))


def yz_groups():
    return [
        [index_of(x_hi, z, core, y, x_lo) for z in range(NZ) for y in range(NY)]
        for x_hi in range(NX_HI)
        for core in range(2)
        for x_lo in range(NX_LO)
    ]


def gather_weights(block):
    shape = block.shape[:3] + (3 * HALF_HEADS * HD,)
    whole = lax.all_gather(
        block.reshape(-1, shape[-1]), AXES, axis=0, tiled=True, axis_index_groups=yz_groups()
    )
    return whole.reshape(NZ * NY, *shape)


def held_back(arrays, *others):
    return lax.optimization_barrier((tuple(arrays), others))[0]


def columns(w_ref):
    blocks = [
        w_ref[z * NY + y, x_hi, core]
        for x_hi in range(NX_HI)
        for z in range(NZ)
        for core in range(2)
        for y in range(NY)
    ]
    return jnp.concatenate(blocks, axis=0)


def head_norm(block, gain_ref):
    square = jnp.mean(block * block, axis=-1, keepdims=True)
    return (block * lax.rsqrt(square + 1e-06) * gain_ref[...]).astype(BF16)


def weight_specs(parts, index):
    return [
        pl.BlockSpec(
            (NZ * NY, NX_HI, 2, 48, PAIR),
            lambda *ids, part=part: (0, 0, 0, 0, part * PAIRS + index(*ids)),
        )
        for part in parts
    ]


def project_kernel(with_query, place_ref, q_gain_ref, k_gain_ref, *refs):
    weights = refs[: 2 + with_query]
    tokens = refs[2 + with_query : 10 + with_query]
    k_ref, v_ref, up_ref, down_ref = refs[10 + with_query : 14 + with_query]
    q_ref = refs[14 + with_query] if with_query else None
    xs, x_sem = refs[-2:]
    core, x_lo = place_ref[0], place_ref[3]
    pair, group = pl.program_id(0), pl.program_id(1)

    @pl.when((pair == 0) & (group == 0))
    def _():
        edge, inner = 3 * core, 1 + core
        rows = (edge, 3 - edge, inner, 3 - inner)
        for t, source in enumerate(tokens):
            row = rows[t // 2]
            beside = t % 2 == 0
            if with_query:
                at = row * 2 + (1 - x_lo if beside else x_lo)
            else:
                at = (1 - x_lo if beside else x_lo) * 4 + row
            pltpu.make_async_copy(source, xs.at[at], x_sem.at[at]).start()

    @pl.when(pair == 0)
    def _():
        for t in range(4):
            at = group * 4 + t
            pltpu.make_async_copy(xs.at[at], xs.at[at], x_sem.at[at]).wait()

    def project(w_ref):
        x = xs[pl.ds(group * 4, 4)].reshape(4 * TOK, D)
        return jnp.dot(x, columns(w_ref), preferred_element_type=F32)

    key, value = project(weights[0]), project(weights[1])
    query = project(weights[2]) if with_query else None
    for h in range(2):
        of_head = slice(h * HD, (h + 1) * HD)
        keys = head_norm(key[:, of_head], k_gain_ref).reshape(4, TOK, HD)
        values = value[:, of_head].astype(BF16).reshape(4, TOK, HD)
        k_ref[0, :, h] = keys
        v_ref[0, :, h] = values
        if with_query:
            q_ref[0, :, h] = head_norm(query[:, of_head], q_gain_ref).reshape(4, TOK, HD)

            @pl.when(group == 0)
            def _():
                up_ref[0, 0, :, h] = keys[:2]
                up_ref[0, 1, :, h] = values[:2]

            @pl.when(group == 1)
            def _():
                down_ref[0, 0, :, h] = keys[2:]
                down_ref[0, 1, :, h] = values[2:]
        else:
            up_ref[0, 0, group, h] = keys[0]
            up_ref[0, 1, group, h] = values[0]
            down_ref[0, 0, group, h] = keys[3]
            down_ref[0, 1, group, h] = values[3]


def project(with_query, place, q_gain, k_gain, weights, tokens):
    smem = pl.BlockSpec(memory_space=pltpu.SMEM)
    vmem = pl.BlockSpec(memory_space=pltpu.VMEM)
    parts = (1, 2, 0) if with_query else (1, 2)
    tiles = jax.ShapeDtypeStruct((PAIRS, 8, 2, TOK, HD), BF16)
    packed = jax.ShapeDtypeStruct((PAIRS, 2, 2, 2, TOK, HD), BF16)
    tile_spec = pl.BlockSpec((1, 4, 2, TOK, HD), lambda j, g: (j, g, 0, 0, 0))
    packed_spec = pl.BlockSpec((1, 2, 2, 2, TOK, HD), lambda j, g: (j, 0, 0, 0, 0, 0))
    return pl.pallas_call(
        functools.partial(project_kernel, with_query),
        grid=(PAIRS, 2),
        in_specs=[smem, vmem, vmem]
        + weight_specs(parts, lambda j, g: j)
        + [pl.BlockSpec(memory_space=pl.ANY)] * 8,
        out_specs=[tile_spec, tile_spec, packed_spec, packed_spec] + [tile_spec] * with_query,
        out_shape=[tiles, tiles, packed, packed] + [tiles] * with_query,
        scratch_shapes=[pltpu.VMEM((8, TOK, D), BF16), pltpu.SemaphoreType.DMA((8,))],
        compiler_params=pltpu.CompilerParams(vmem_limit_bytes=60 * MIB),
        cost_estimate=pl.CostEstimate(
            flops=2 * 8 * TOK * D * PAIRS * PAIR * len(parts),
            bytes_accessed=30 * 10**6,
            transcendentals=10**5,
        ),
        name="project",
    )(place, q_gain, k_gain, *[weights] * len(parts), *tokens)


def attend_kernel(edges, place_ref, radii_ref, q_ref, k_ref, v_ref, k_sides, v_sides, *refs):
    ends, (send_ref, keep_ref) = refs[:-2], refs[-2:]
    core, row, col = (place_ref[i] for i in range(3))
    pair = pl.program_id(0)
    factor = math.log2(math.e) / math.sqrt(HD)

    def tile_of(middle, sides, which, r, c, h):
        if 1 <= r <= 4:
            if c in (1, 2):
                return middle[0, 2 * (r - 1) + c - 1, h]
            return sides[0, c // 3 * 4 + r - 1, h]
        end = (0 if r == 0 else 1) + (0 if c in (1, 2) else 2)
        return ends[end][0, which, c - 1 if c in (1, 2) else c // 3, h]

    def row_of(middle, sides, which, r, c, h):
        tiles = [tile_of(middle, sides, which, r, c + dc, h) for dc in (-1, 0, 1)]
        return jnp.concatenate(tiles, axis=0)

    def attend_tile(r, c, h):
        reach = core * HALF_HEADS + pair * 2 + h
        reach_r, reach_c = radii_ref[reach, 0], radii_ref[reach, 1]
        q = q_ref[0, 2 * (r - 1) + c - 1, h]
        scores, hidden = [], []
        top = None
        for dr in (-1, 0, 1):
            k = row_of(k_ref, k_sides, 0, r + dr, c, h)
            score = lax.dot_general(q, k, (((1,), (1,)), ((), ())), preferred_element_type=F32)
            for dc in (-1, 0, 1):
                block = score[:, (dc + 1) * TOK : (dc + 2) * TOK]
                tile_r, tile_c = row * 4 + r - 1 + dr, col * 2 + c - 1 + dc
                seen = (
                    (abs(dr) <= reach_r)
                    & (abs(dc) <= reach_c)
                    & (tile_r >= 0)
                    & (tile_r < 4 * ROWS_OF_CHIPS)
                    & (tile_c >= 0)
                    & (tile_c < 2 * COLS_OF_CHIPS)
                )
                offset = jnp.where(seen, 0.0, 1e30).astype(F32)
                scores.append(block)
                hidden.append(offset)
                shown = block - offset
                top = shown if top is None else jnp.maximum(top, shown)
        peak = jnp.max(top, axis=-1, keepdims=True) * factor
        total = None
        mixed = None
        for j, dr in enumerate((-1, 0, 1)):
            weights = []
            for i in range(3):
                n = 3 * j + i
                prob = jnp.exp2(scores[n] * factor - (peak + hidden[n]))
                total = prob if total is None else total + prob
                weights.append(prob.astype(BF16))
            v = row_of(v_ref, v_sides, 1, r + dr, c, h)
            term = jnp.dot(jnp.concatenate(weights, axis=1), v, preferred_element_type=F32)
            mixed = term if mixed is None else mixed + term
        den = jnp.sum(total, axis=-1, keepdims=True)
        return (mixed / den).astype(BF16)

    rows = (1, 4) if edges else (2, 3)
    for h in range(2):
        of_head = slice(h * HD, (h + 1) * HD)
        for c in (1, 2):
            low, high = (attend_tile(r, c, h) for r in rows)
            send_ref[c - 1, :, of_head] = jnp.where(core == 0, high, low)
            keep_ref[c - 1, :, of_head] = jnp.where(core == 0, low, high)


def attend(edges, place, radii, arrays):
    smem = pl.BlockSpec(memory_space=pltpu.SMEM)
    shape = jax.ShapeDtypeStruct((2, TOK, HALF_HEADS * HD), BF16)
    out = pl.BlockSpec((2, TOK, PAIR), lambda j: (0, 0, j))
    tiles = pl.BlockSpec((1, 8, 2, TOK, HD), lambda j: (j, 0, 0, 0, 0))
    packed = pl.BlockSpec((1, 2, 2, 2, TOK, HD), lambda j: (j, 0, 0, 0, 0, 0))
    return pl.pallas_call(
        functools.partial(attend_kernel, edges),
        grid=(PAIRS,),
        in_specs=[smem, smem] + [tiles] * 5 + [packed] * (len(arrays) - 5),
        out_specs=[out, out],
        out_shape=[shape, shape],
        compiler_params=pltpu.CompilerParams(vmem_limit_bytes=60 * MIB),
        cost_estimate=pl.CostEstimate(
            flops=7 * 10**9, bytes_accessed=15 * 10**6, transcendentals=4 * 10**6
        ),
        name="attend",
    )(place, radii, *arrays)


def assemble_kernel(place_ref, *refs):
    core = place_ref[0]
    inner_keep, inner_got, edge_keep, edge_got, out_ref = refs
    inner = pl.program_id(0) != core
    width = HALF_HEADS * HD

    def rows(inner_ref, edge_ref):
        halves = [
            jnp.where(inner, inner_ref[c, 0].astype(F32), edge_ref[c, 0].astype(F32))
            for c in range(2)
        ]
        return jnp.concatenate([half.reshape(8, 8, width) for half in halves], axis=1)

    mine, got = rows(inner_keep, edge_keep), rows(inner_got, edge_got)
    out_ref[0, :, :, :width] = jnp.where(core == 0, mine, got).astype(BF16)
    out_ref[0, :, :, width:] = jnp.where(core == 0, got, mine).astype(BF16)


def assemble(place, arrays):
    width = HALF_HEADS * HD
    tiles = pl.BlockSpec((2, 1, 64, width), lambda t, f: (0, f, 0, 0))
    return pl.pallas_call(
        assemble_kernel,
        grid=(2, 2),
        in_specs=[pl.BlockSpec(memory_space=pltpu.SMEM)] + [tiles] * 4,
        out_specs=pl.BlockSpec((1, 8, 16, 2 * width), lambda t, f: (f, t, 0, 0)),
        out_shape=jax.ShapeDtypeStruct((2, 16, 16, 2 * width), BF16),
        name="assemble",
    )(place, *[a.reshape(2, 2, 64, width) for a in arrays])


def local(latents, cond_mask, radii, cond_embed, mod_shift, mod_scale, w_qkv, q_gain, k_gain):
    ha, wa = lax.axis_index("ha"), lax.axis_index("wa")
    core, row = ha % 2, ha // 2
    x_hi, x_lo = row // NZ, wa % NX_LO
    place = jnp.stack([core, row, wa, x_lo]).astype(jnp.int32)
    gains = q_gain.reshape(1, HD), k_gain.reshape(1, HD)

    def swap(*arrays):
        return tuple(send(a, swap_core) for a in arrays)

    norm_args = (x_lo, latents, cond_mask.astype(F32)[..., None], cond_embed, mod_shift, mod_scale)
    edges = normalize(core, *norm_args)
    block = x_block(w_qkv, core, x_lo, x_hi, edges[0])

    diagonal_edge = send(edges[1], swap_diagonal)
    (block,) = held_back((block,), diagonal_edge)
    weights = gather_weights(block)
    inners = normalize(1 - core, *norm_args)
    middle = edges + swap(*edges) + inners + swap(*inners)
    edge_near, inner_near = held_back((edges[0], inners[0]), block, *middle)
    beside_edge, beside_inner = send(edge_near, swap_beside), send(inner_near, swap_beside)
    (inner_far,) = held_back(inners[1:], weights)
    diagonal_inner = send(inner_far, swap_diagonal)

    def exchange_rows(up, down):
        return send(down, next_row(1)), send(up, next_row(-1))

    key, value, up, down, query = project(True, place, *gains, weights, middle)
    ends = exchange_rows(up, down)
    (diagonal_inner,) = held_back((diagonal_inner,), query)
    edges, inners = (beside_edge, diagonal_edge), (beside_inner, diagonal_inner)
    sides = edges + swap(*edges) + inners + swap(*inners)
    key_sides, value_sides, up, down = project(False, place, *gains, weights, sides)
    ends += exchange_rows(up, down)
    arrays = (query, key, value, key_sides, value_sides)
    inner_away, inner_keep = attend(False, place, radii, arrays)
    (inner_got,) = swap(inner_away)
    edge_away, edge_keep = attend(True, place, radii, arrays + ends)
    (edge_got,) = swap(edge_away)
    return assemble(place, (inner_keep, inner_got, edge_keep, edge_got))


def solution(mesh):
    in_specs = (
        P(None, "ha", "wa", None),
        P(None, "ha", "wa"),
        P(),
        P(),
        P(),
        P(),
        P(("ha", "wa"), None),
        P(),
        P(),
    )
    out_specs = P(None, "ha", "wa", None)
    return jax.shard_map(local, mesh=mesh, in_specs=in_specs, out_specs=out_specs, check_vma=False)
```

```python
import functools
import math

import jax
import jax.numpy as jnp
from jax import lax
from jax.experimental import pallas as pl
from jax.experimental.pallas import tpu as pltpu
from jax.sharding import PartitionSpec as P

AXES = ("ha", "wa")
NX_HI, NZ, NY, NX_LO = 2, 4, 4, 2
ROWS_OF_CHIPS, COLS_OF_CHIPS = NX_HI * NZ, NY * NX_LO
F32, BF16 = jnp.float32, jnp.bfloat16
D, HD, TOK = 3072, 128, 128
HALF_HEADS, PAIRS = 6, 3
PAIR = 2 * HD
MIB = 1024 * 1024


def index_of(x_hi, z, core, y, x_lo):
    return ((x_hi * NZ + z) * 2 + core) * COLS_OF_CHIPS + y * NX_LO + x_lo


def permutation(move):
    pairs = []
    for x_hi in range(NX_HI):
        for z in range(NZ):
            for core in range(2):
                for y in range(NY):
                    for x_lo in range(NX_LO):
                        target = move(x_hi, z, core, y, x_lo)
                        if target is not None:
                            pairs.append((index_of(x_hi, z, core, y, x_lo), index_of(*target)))
    return pairs


def swap_core(x_hi, z, core, y, x_lo):
    return x_hi, z, 1 - core, y, x_lo


def flip_x(bits):
    return lambda x_hi, z, core, y, x_lo: (x_hi ^ (bits >> 1), z, core, y, x_lo ^ (bits & 1))


def swap_beside(x_hi, z, core, y, x_lo):
    return x_hi, z, core, y, 1 - x_lo


def swap_diagonal(x_hi, z, core, y, x_lo):
    wa = y * NX_LO + x_lo + (1 if x_lo else -1)
    if not 0 <= wa < COLS_OF_CHIPS:
        return None
    return x_hi, z, core, wa // NX_LO, wa % NX_LO


def next_row(by):
    def move(x_hi, z, core, y, x_lo):
        q = x_hi * NZ + z + by
        if not 0 <= q < ROWS_OF_CHIPS:
            return None
        return q // NZ, q % NZ, core, y, x_lo

    return move


def send(array, move):
    return lax.ppermute(array, AXES, permutation(move))


def norm_kernel(place_ref, lat_ref, mask_ref, embed_ref, shift_ref, scale_ref, near_ref, far_ref):
    cond = lat_ref[0].astype(F32) + mask_ref[0] * embed_ref[...]
    center = cond - jnp.mean(cond, axis=-1, keepdims=True)
    spread = jnp.mean(center * center, axis=-1, keepdims=True)
    normed = center * lax.rsqrt(spread + 1e-06) * (1.0 + scale_ref[...]) + shift_ref[...]
    left, right = normed[:, :8].reshape(64, D), normed[:, 8:].reshape(64, D)
    first = place_ref[1] == 0
    near_ref[0] = jnp.where(first, right, left).astype(BF16)
    far_ref[0] = jnp.where(first, left, right).astype(BF16)


def normalize(tile_row, x_lo, latents, mask, cond_embed, mod_shift, mod_scale):
    vector = pl.BlockSpec((1, 1, D), lambda f, t: (0, 0, 0))
    tile = pl.BlockSpec((1, 64, D), lambda f, t: (f, 0, 0))
    shape = jax.ShapeDtypeStruct((2, 64, D), BF16)
    left, right = pl.pallas_call(
        norm_kernel,
        grid_spec=pltpu.PrefetchScalarGridSpec(
            num_scalar_prefetch=1,
            grid=(2,),
            in_specs=[
                pl.BlockSpec((1, 8, 16, D), lambda f, t: (f, t[0], 0, 0)),
                pl.BlockSpec((1, 8, 16, 1), lambda f, t: (f, t[0], 0, 0)),
                vector,
                vector,
                vector,
            ],
            out_specs=[tile, tile],
        ),
        out_shape=[shape, shape],
        compiler_params=pltpu.CompilerParams(vmem_limit_bytes=48 * MIB),
        name="norm",
    )(
        jnp.stack([tile_row, x_lo]).astype(jnp.int32),
        latents,
        mask,
        cond_embed.reshape(1, 1, D),
        mod_shift.reshape(1, 1, D),
        mod_scale.reshape(1, 1, D),
    )
    return left.reshape(TOK, D), right.reshape(TOK, D)


def x_block(w_qkv, core, x_lo, x_hi):
    rows = w_qkv.shape[0]
    split = w_qkv.reshape(rows, 3, 2, HALF_HEADS * HD)
    first, second = split[:, :, 0], split[:, :, 1]
    mine = jnp.where(core == 0, first, second)
    theirs = jnp.where(core == 0, second, first)
    got = send(theirs, swap_core)
    both = jnp.where(core == 0, jnp.stack([mine, got]), jnp.stack([got, mine]))
    flips = [both] + [send(both, flip_x(bits)) for bits in (1, 2, 3)]

    def pair(same, other):
        return jnp.where(
            x_lo == 0,
            jnp.concatenate([same, other], axis=1),
            jnp.concatenate([other, same], axis=1),
        )

    here, there = pair(flips[0], flips[1]), pair(flips[2], flips[3])
    return jnp.where(x_hi == 0, jnp.stack([here, there]), jnp.stack([there, here]))


def yz_groups():
    return [
        [index_of(x_hi, z, core, y, x_lo) for z in range(NZ) for y in range(NY)]
        for x_hi in range(NX_HI)
        for core in range(2)
        for x_lo in range(NX_LO)
    ]


def gather_weights(block):
    shape = block.shape[:3] + (3 * HALF_HEADS * HD,)
    whole = lax.all_gather(
        block.reshape(-1, shape[-1]), AXES, axis=0, tiled=True, axis_index_groups=yz_groups()
    )
    return whole.reshape(NZ * NY, *shape)


def held_back(arrays, *others):
    return lax.optimization_barrier((tuple(arrays), others))[0]


def columns(w_ref):
    blocks = [
        w_ref[z * NY + y, x_hi, core]
        for x_hi in range(NX_HI)
        for z in range(NZ)
        for core in range(2)
        for y in range(NY)
    ]
    return jnp.concatenate(blocks, axis=0)


def head_norm(block, gain_ref):
    square = jnp.mean(block * block, axis=-1, keepdims=True)
    return (block * lax.rsqrt(square + 1e-06) * gain_ref[...]).astype(BF16)


def weight_specs(parts, index):
    return [
        pl.BlockSpec(
            (NZ * NY, NX_HI, 2, 48, PAIR),
            lambda *ids, part=part: (0, 0, 0, 0, part * PAIRS + index(*ids)),
        )
        for part in parts
    ]


def project_kernel(with_query, place_ref, q_gain_ref, k_gain_ref, *refs):
    weights = refs[: 2 + with_query]
    tokens = refs[2 + with_query : 10 + with_query]
    k_ref, v_ref, up_ref, down_ref = refs[10 + with_query : 14 + with_query]
    q_ref = refs[14 + with_query] if with_query else None
    xs, x_sem = refs[-2:]
    core, x_lo = place_ref[0], place_ref[3]
    pair, group = pl.program_id(0), pl.program_id(1)

    @pl.when((pair == 0) & (group == 0))
    def _():
        edge, inner = 3 * core, 1 + core
        rows = (edge, 3 - edge, inner, 3 - inner)
        for t, source in enumerate(tokens):
            row = rows[t // 2]
            beside = t % 2 == 0
            if with_query:
                at = row * 2 + (1 - x_lo if beside else x_lo)
            else:
                at = (1 - x_lo if beside else x_lo) * 4 + row
            pltpu.make_async_copy(source, xs.at[at], x_sem.at[at]).start()

    @pl.when(pair == 0)
    def _():
        for t in range(4):
            at = group * 4 + t
            pltpu.make_async_copy(xs.at[at], xs.at[at], x_sem.at[at]).wait()

    def project(w_ref):
        x = xs[pl.ds(group * 4, 4)].reshape(4 * TOK, D)
        return jnp.dot(x, columns(w_ref), preferred_element_type=F32)

    key, value = project(weights[0]), project(weights[1])
    query = project(weights[2]) if with_query else None
    for h in range(2):
        of_head = slice(h * HD, (h + 1) * HD)
        keys = head_norm(key[:, of_head], k_gain_ref).reshape(4, TOK, HD)
        values = value[:, of_head].astype(BF16).reshape(4, TOK, HD)
        k_ref[0, :, h] = keys
        v_ref[0, :, h] = values
        if with_query:
            q_ref[0, :, h] = head_norm(query[:, of_head], q_gain_ref).reshape(4, TOK, HD)

            @pl.when(group == 0)
            def _():
                up_ref[0, 0, :, h] = keys[:2]
                up_ref[0, 1, :, h] = values[:2]

            @pl.when(group == 1)
            def _():
                down_ref[0, 0, :, h] = keys[2:]
                down_ref[0, 1, :, h] = values[2:]
        else:
            up_ref[0, 0, group, h] = keys[0]
            up_ref[0, 1, group, h] = values[0]
            down_ref[0, 0, group, h] = keys[3]
            down_ref[0, 1, group, h] = values[3]


def project(with_query, place, q_gain, k_gain, weights, tokens):
    smem = pl.BlockSpec(memory_space=pltpu.SMEM)
    vmem = pl.BlockSpec(memory_space=pltpu.VMEM)
    parts = (1, 2, 0) if with_query else (1, 2)
    tiles = jax.ShapeDtypeStruct((PAIRS, 8, 2, TOK, HD), BF16)
    packed = jax.ShapeDtypeStruct((PAIRS, 2, 2, 2, TOK, HD), BF16)
    tile_spec = pl.BlockSpec((1, 4, 2, TOK, HD), lambda j, g: (j, g, 0, 0, 0))
    packed_spec = pl.BlockSpec((1, 2, 2, 2, TOK, HD), lambda j, g: (j, 0, 0, 0, 0, 0))
    return pl.pallas_call(
        functools.partial(project_kernel, with_query),
        grid=(PAIRS, 2),
        in_specs=[smem, vmem, vmem]
        + weight_specs(parts, lambda j, g: j)
        + [pl.BlockSpec(memory_space=pl.ANY)] * 8,
        out_specs=[tile_spec, tile_spec, packed_spec, packed_spec] + [tile_spec] * with_query,
        out_shape=[tiles, tiles, packed, packed] + [tiles] * with_query,
        scratch_shapes=[pltpu.VMEM((8, TOK, D), BF16), pltpu.SemaphoreType.DMA((8,))],
        compiler_params=pltpu.CompilerParams(vmem_limit_bytes=60 * MIB),
        cost_estimate=pl.CostEstimate(
            flops=2 * 8 * TOK * D * PAIRS * PAIR * len(parts),
            bytes_accessed=30 * 10**6,
            transcendentals=10**5,
        ),
        name="project",
    )(place, q_gain, k_gain, *[weights] * len(parts), *tokens)


def attend_kernel(edges, place_ref, radii_ref, q_ref, k_ref, v_ref, k_sides, v_sides, *refs):
    ends, (send_ref, keep_ref) = refs[:-2], refs[-2:]
    core, row, col = (place_ref[i] for i in range(3))
    pair = pl.program_id(0)
    factor = math.log2(math.e) / math.sqrt(HD)

    def tile_of(middle, sides, which, r, c, h):
        if 1 <= r <= 4:
            if c in (1, 2):
                return middle[0, 2 * (r - 1) + c - 1, h]
            return sides[0, c // 3 * 4 + r - 1, h]
        end = (0 if r == 0 else 1) + (0 if c in (1, 2) else 2)
        return ends[end][0, which, c - 1 if c in (1, 2) else c // 3, h]

    def row_of(middle, sides, which, r, h, cols):
        tiles = [tile_of(middle, sides, which, r, c, h) for c in cols]
        return jnp.concatenate(tiles, axis=0)

    def scores_of(r, h, reach_r, reach_c):
        q = jnp.concatenate([q_ref[0, 2 * (r - 1) + i, h] for i in range(2)], axis=0)
        rows, cols = range(r - reach_r, r + reach_r + 1), range(1 - reach_c, 3 + reach_c)
        return [
            lax.dot_general(
                q,
                row_of(k_ref, k_sides, 0, at, h, cols),
                (((1,), (1,)), ((), ())),
                preferred_element_type=F32,
            )
            for at in rows
        ]

    def weights_of(scores, r, reach_r, reach_c):
        rows, cols = range(r - reach_r, r + reach_r + 1), range(1 - reach_c, 3 + reach_c)
        probs, dens = [], []
        for i in range(2):
            shown, top = [], None
            for j, at in enumerate(rows):
                for c in range(1 + i - reach_c, 2 + i + reach_c):
                    n = c - cols[0]
                    block = scores[j][i * TOK : (i + 1) * TOK, n * TOK : (n + 1) * TOK]
                    tile_r, tile_c = row * 4 + at - 1, col * 2 + c - 1
                    inside = (
                        (tile_r >= 0)
                        & (tile_r < 4 * ROWS_OF_CHIPS)
                        & (tile_c >= 0)
                        & (tile_c < 2 * COLS_OF_CHIPS)
                    )
                    offset = jnp.where(inside, 0.0, 1e30).astype(F32)
                    shown.append((j, n, block, offset))
                    if 1 <= at <= 4 and c in (1, 2):
                        seen = block
                    else:
                        seen = block - offset
                    top = seen if top is None else jnp.maximum(top, seen)
            peak = jnp.max(top, axis=-1, keepdims=True) * factor
            total = None
            prob = [[jnp.zeros((TOK, TOK), BF16)] * len(cols) for _ in rows]
            for j, n, block, offset in shown:
                weight = jnp.exp2(block * factor - (peak + offset))
                total = weight if total is None else total + weight
                prob[j][n] = weight.astype(BF16)
            probs.append(prob)
            dens.append(jnp.sum(total, axis=-1, keepdims=True))
        return probs, dens

    def mixed_of(probs, dens, r, h, reach_r, reach_c):
        rows, cols = range(r - reach_r, r + reach_r + 1), range(1 - reach_c, 3 + reach_c)
        mixed = None
        for j, at in enumerate(rows):
            weights = [jnp.concatenate(probs[i][j], axis=1) for i in range(2)]
            term = jnp.dot(
                jnp.concatenate(weights, axis=0),
                row_of(v_ref, v_sides, 1, at, h, cols),
                preferred_element_type=F32,
            )
            mixed = term if mixed is None else mixed + term
        return [(mixed[i * TOK : (i + 1) * TOK] / dens[i]).astype(BF16) for i in range(2)]

    def attend_heads(heads, reach_r, reach_c):
        reach = reach_r, reach_c
        both = [(r, h) for h in heads for r in ((1, 4) if edges else (2, 3))]
        scores = [scores_of(r, h, *reach) for r, h in both]
        weights = [weights_of(score, r, *reach) for score, (r, h) in zip(scores, both)]
        mixed = [mixed_of(*weight, r, h, *reach) for weight, (r, h) in zip(weights, both)]
        for n, h in enumerate(heads):
            low, high = mixed[2 * n : 2 * n + 2]
            of_head = slice(h * HD, (h + 1) * HD)
            for c in range(2):
                send_ref[c, :, of_head] = jnp.where(core == 0, high[c], low[c])
                keep_ref[c, :, of_head] = jnp.where(core == 0, low[c], high[c])

    first = core * HALF_HEADS + pair * 2
    wide = [(radii_ref[first + h, 0] == 1) & (radii_ref[first + h, 1] == 1) for h in range(2)]
    pl.when(wide[0] & wide[1])(functools.partial(attend_heads, (0, 1), 1, 1))

    @pl.when(~(wide[0] & wide[1]))
    def _():
        for h in range(2):
            for reach_r in (0, 1):
                for reach_c in (0, 1):
                    taken = (radii_ref[first + h, 0] == reach_r) & (
                        radii_ref[first + h, 1] == reach_c
                    )
                    pl.when(taken)(functools.partial(attend_heads, (h,), reach_r, reach_c))


def attend(edges, place, radii, arrays):
    smem = pl.BlockSpec(memory_space=pltpu.SMEM)
    shape = jax.ShapeDtypeStruct((2, TOK, HALF_HEADS * HD), BF16)
    out = pl.BlockSpec((2, TOK, PAIR), lambda j: (0, 0, j))
    tiles = pl.BlockSpec((1, 8, 2, TOK, HD), lambda j: (j, 0, 0, 0, 0))
    packed = pl.BlockSpec((1, 2, 2, 2, TOK, HD), lambda j: (j, 0, 0, 0, 0, 0))
    return pl.pallas_call(
        functools.partial(attend_kernel, edges),
        grid=(PAIRS,),
        in_specs=[smem, smem] + [tiles] * 5 + [packed] * (len(arrays) - 5),
        out_specs=[out, out],
        out_shape=[shape, shape],
        compiler_params=pltpu.CompilerParams(vmem_limit_bytes=60 * MIB),
        cost_estimate=pl.CostEstimate(
            flops=7 * 10**9, bytes_accessed=15 * 10**6, transcendentals=4 * 10**6
        ),
        name="attend",
    )(place, radii, *arrays)


def assemble_kernel(place_ref, keep_ref, got_ref, *refs):
    first = place_ref[0] == 0
    out_ref = refs[-1]
    width = HALF_HEADS * HD

    def rows(ref):
        halves = [ref[c, 0].astype(F32).reshape(8, 8, width) for c in range(2)]
        return jnp.concatenate(halves, axis=1)

    mine, got = rows(keep_ref), rows(got_ref)
    out_ref[0, :, :, :width] = jnp.where(first, mine, got).astype(BF16)
    out_ref[0, :, :, width:] = jnp.where(first, got, mine).astype(BF16)


def assemble(core, tile_row, keep, got, into=None):
    width = HALF_HEADS * HD
    tiles = pl.BlockSpec((2, 1, 64, width), lambda f, t: (0, f, 0, 0))
    others = () if into is None else (into,)
    return pl.pallas_call(
        assemble_kernel,
        grid_spec=pltpu.PrefetchScalarGridSpec(
            num_scalar_prefetch=1,
            grid=(2,),
            in_specs=[tiles, tiles] + [pl.BlockSpec(memory_space=pl.ANY)] * len(others),
            out_specs=pl.BlockSpec((1, 8, 16, 2 * width), lambda f, t: (f, t[1], 0, 0)),
        ),
        out_shape=jax.ShapeDtypeStruct((2, 16, 16, 2 * width), BF16),
        input_output_aliases={3: 0} if others else {},
        name="assemble",
    )(
        jnp.stack([core, tile_row]).astype(jnp.int32),
        *[a.reshape(2, 2, 64, width) for a in (keep, got)],
        *others,
    )


def local(latents, cond_mask, radii, cond_embed, mod_shift, mod_scale, w_qkv, q_gain, k_gain):
    ha, wa = lax.axis_index("ha"), lax.axis_index("wa")
    core, row = ha % 2, ha // 2
    x_hi, x_lo = row // NZ, wa % NX_LO
    place = jnp.stack([core, row, wa, x_lo]).astype(jnp.int32)
    gains = q_gain.reshape(1, HD), k_gain.reshape(1, HD)

    def swap(*arrays):
        return tuple(send(a, swap_core) for a in arrays)

    norm_args = (x_lo, latents, cond_mask.astype(F32)[..., None], cond_embed, mod_shift, mod_scale)
    block = x_block(w_qkv, core, x_lo, x_hi)
    weights = gather_weights(block)
    edges, inners = normalize(core, *norm_args), normalize(1 - core, *norm_args)
    middle = edges + swap(*edges) + inners + swap(*inners)

    edge_near, inner_near = held_back((edges[0], inners[0]), block, *middle)
    beside_edge, beside_inner = send(edge_near, swap_beside), send(inner_near, swap_beside)
    edge_far, inner_far = held_back((edges[1], inners[1]), weights)
    diagonal_edge, diagonal_inner = send(edge_far, swap_diagonal), send(inner_far, swap_diagonal)

    def exchange_rows(up, down):
        return send(down, next_row(1)), send(up, next_row(-1))

    key, value, up, down, query = project(True, place, *gains, weights, middle)
    ends = exchange_rows(up, down)
    diagonal_edge, diagonal_inner = held_back((diagonal_edge, diagonal_inner), query)
    edges, inners = (beside_edge, diagonal_edge), (beside_inner, diagonal_inner)
    sides = edges + swap(*edges) + inners + swap(*inners)
    key_sides, value_sides, up, down = project(False, place, *gains, weights, sides)
    ends += exchange_rows(up, down)
    arrays = (query, key, value, key_sides, value_sides)
    inner_away, inner_keep = attend(False, place, radii, arrays)
    (inner_got,) = swap(inner_away)
    out = assemble(core, 1 - core, inner_keep, inner_got)
    ends = held_back(ends, out)
    edge_away, edge_keep = attend(True, place, radii, arrays + ends)
    (edge_got,) = swap(edge_away)
    return assemble(core, core, edge_keep, edge_got, out)


def solution(mesh):
    in_specs = (
        P(None, "ha", "wa", None),
        P(None, "ha", "wa"),
        P(),
        P(),
        P(),
        P(),
        P(("ha", "wa"), None),
        P(),
        P(),
    )
    out_specs = P(None, "ha", "wa", None)
    return jax.shard_map(local, mesh=mesh, in_specs=in_specs, out_specs=out_specs, check_vma=False)
```

```python
import functools
import math

import jax
import jax.numpy as jnp
from jax import lax
from jax.experimental import pallas as pl
from jax.experimental.pallas import tpu as pltpu
from jax.sharding import PartitionSpec as P

AXES = ("ha", "wa")
NX_HI, NZ, NY, NX_LO = 2, 4, 4, 2
ROWS_OF_CHIPS, COLS_OF_CHIPS = NX_HI * NZ, NY * NX_LO
F32, BF16 = jnp.float32, jnp.bfloat16
D, HD, TOK = 3072, 128, 128
HALF_HEADS, PAIRS = 6, 3
PAIR = 2 * HD
MIB = 1024 * 1024


def index_of(x_hi, z, core, y, x_lo):
    return ((x_hi * NZ + z) * 2 + core) * COLS_OF_CHIPS + y * NX_LO + x_lo


def permutation(move):
    pairs = []
    for x_hi in range(NX_HI):
        for z in range(NZ):
            for core in range(2):
                for y in range(NY):
                    for x_lo in range(NX_LO):
                        target = move(x_hi, z, core, y, x_lo)
                        if target is not None:
                            pairs.append((index_of(x_hi, z, core, y, x_lo), index_of(*target)))
    return pairs


def swap_core(x_hi, z, core, y, x_lo):
    return x_hi, z, 1 - core, y, x_lo


def flip_x(bits):
    return lambda x_hi, z, core, y, x_lo: (x_hi ^ (bits >> 1), z, core, y, x_lo ^ (bits & 1))


def swap_beside(x_hi, z, core, y, x_lo):
    return x_hi, z, core, y, 1 - x_lo


def swap_diagonal(x_hi, z, core, y, x_lo):
    wa = y * NX_LO + x_lo + (1 if x_lo else -1)
    if not 0 <= wa < COLS_OF_CHIPS:
        return None
    return x_hi, z, core, wa // NX_LO, wa % NX_LO


def next_row(by):
    def move(x_hi, z, core, y, x_lo):
        q = x_hi * NZ + z + by
        if not 0 <= q < ROWS_OF_CHIPS:
            return None
        return q // NZ, q % NZ, core, y, x_lo

    return move


def send(array, move):
    return lax.ppermute(array, AXES, permutation(move))


def norm_kernel(place_ref, lat_ref, mask_ref, embed_ref, shift_ref, scale_ref, near_ref, far_ref):
    cond = lat_ref[0].astype(F32) + mask_ref[0] * embed_ref[...]
    center = cond - jnp.mean(cond, axis=-1, keepdims=True)
    spread = jnp.mean(center * center, axis=-1, keepdims=True)
    normed = center * lax.rsqrt(spread + 1e-06) * (1.0 + scale_ref[...]) + shift_ref[...]
    left, right = normed[:, :8].reshape(64, D), normed[:, 8:].reshape(64, D)
    first = place_ref[1] == 0
    near_ref[0] = jnp.where(first, right, left).astype(BF16)
    far_ref[0] = jnp.where(first, left, right).astype(BF16)


def normalize(tile_row, x_lo, latents, mask, cond_embed, mod_shift, mod_scale):
    vector = pl.BlockSpec((1, 1, D), lambda f, t: (0, 0, 0))
    tile = pl.BlockSpec((1, 64, D), lambda f, t: (f, 0, 0))
    shape = jax.ShapeDtypeStruct((2, 64, D), BF16)
    left, right = pl.pallas_call(
        norm_kernel,
        grid_spec=pltpu.PrefetchScalarGridSpec(
            num_scalar_prefetch=1,
            grid=(2,),
            in_specs=[
                pl.BlockSpec((1, 8, 16, D), lambda f, t: (f, t[0], 0, 0)),
                pl.BlockSpec((1, 8, 16, 1), lambda f, t: (f, t[0], 0, 0)),
                vector,
                vector,
                vector,
            ],
            out_specs=[tile, tile],
        ),
        out_shape=[shape, shape],
        compiler_params=pltpu.CompilerParams(vmem_limit_bytes=48 * MIB),
        name="norm",
    )(
        jnp.stack([tile_row, x_lo]).astype(jnp.int32),
        latents,
        mask,
        cond_embed.reshape(1, 1, D),
        mod_shift.reshape(1, 1, D),
        mod_scale.reshape(1, 1, D),
    )
    return left.reshape(TOK, D), right.reshape(TOK, D)


def x_block(w_qkv, core, x_lo, x_hi):
    rows = w_qkv.shape[0]
    split = w_qkv.reshape(rows, 3, 2, HALF_HEADS * HD)
    first, second = split[:, :, 0], split[:, :, 1]
    mine = jnp.where(core == 0, first, second)
    theirs = jnp.where(core == 0, second, first)
    got = send(theirs, swap_core)
    both = jnp.where(core == 0, jnp.stack([mine, got]), jnp.stack([got, mine]))
    flips = [both] + [send(both, flip_x(bits)) for bits in (1, 2, 3)]

    def pair(same, other):
        return jnp.where(
            x_lo == 0,
            jnp.concatenate([same, other], axis=1),
            jnp.concatenate([other, same], axis=1),
        )

    here, there = pair(flips[0], flips[1]), pair(flips[2], flips[3])
    return jnp.where(x_hi == 0, jnp.stack([here, there]), jnp.stack([there, here]))


def yz_groups():
    return [
        [index_of(x_hi, z, core, y, x_lo) for z in range(NZ) for y in range(NY)]
        for x_hi in range(NX_HI)
        for core in range(2)
        for x_lo in range(NX_LO)
    ]


def gather_weights(block):
    shape = block.shape[:3] + (3 * HALF_HEADS * HD,)
    whole = lax.all_gather(
        block.reshape(-1, shape[-1]), AXES, axis=0, tiled=True, axis_index_groups=yz_groups()
    )
    return whole.reshape(NZ * NY, *shape)


def held_back(arrays, *others):
    return lax.optimization_barrier((tuple(arrays), others))[0]


def columns(w_ref):
    blocks = [
        w_ref[z * NY + y, x_hi, core]
        for x_hi in range(NX_HI)
        for z in range(NZ)
        for core in range(2)
        for y in range(NY)
    ]
    return jnp.concatenate(blocks, axis=0)


def head_norm(block, gain_ref):
    square = jnp.mean(block * block, axis=-1, keepdims=True)
    return (block * lax.rsqrt(square + 1e-06) * gain_ref[...]).astype(BF16)


def weight_specs(parts, index):
    return [
        pl.BlockSpec(
            (NZ * NY, NX_HI, 2, 48, PAIR),
            lambda *ids, part=part: (0, 0, 0, 0, part * PAIRS + index(*ids)),
        )
        for part in parts
    ]


def project_kernel(with_query, copied, place_ref, q_gain_ref, k_gain_ref, *refs):
    groups = 2 if with_query else 1
    weights, refs = refs[: 2 + with_query], refs[2 + with_query :]
    tokens, refs = refs[: 4 * groups], refs[4 * groups :]
    to_copy, refs = refs[: 2 if copied else 0], refs[2 if copied else 0 :]
    k_ref, v_ref, *end_refs = refs[:4]
    q_ref = refs[4] if with_query else None
    xs, x_sem = refs[-2:]
    core, x_lo = place_ref[0], place_ref[3]
    pair, group = pl.program_id(0), pl.program_id(1)
    width = 2 if with_query else 1

    @pl.when((pair == 0) & (group == 0))
    def _():
        rows = (3 * core, 3 - 3 * core, 1 + core, 2 - core)
        for t, source in enumerate(tokens):
            at = rows[t // width] * width
            if with_query:
                at += 1 - x_lo if t % 2 == 0 else x_lo
            pltpu.make_async_copy(source, xs.at[at], x_sem.at[at]).start()

    @pl.when(pair == 0)
    def _():
        for t in range(4):
            at = group * 4 + t
            pltpu.make_async_copy(xs.at[at], xs.at[at], x_sem.at[at]).wait()

    def project(w_ref):
        x = xs[pl.ds(group * 4, 4)].reshape(4 * TOK, D)
        return jnp.dot(x, columns(w_ref), preferred_element_type=F32)

    def put_end(end, h, keys, values):
        at = 3 * end if width == 1 else 2 * end
        end_refs[end][0, 0, copied:, h] = keys[at : at + width]
        end_refs[end][0, 1, copied:, h] = values[at : at + width]

    key, value = project(weights[0]), project(weights[1])
    query = project(weights[2]) if with_query else None
    for h in range(2):
        of_head = slice(h * HD, (h + 1) * HD)
        keys = head_norm(key[:, of_head], k_gain_ref).reshape(4, TOK, HD)
        values = value[:, of_head].astype(BF16).reshape(4, TOK, HD)
        k_ref[0, :, h] = keys
        v_ref[0, :, h] = values
        if with_query:
            q_ref[0, :, h] = head_norm(query[:, of_head], q_gain_ref).reshape(4, TOK, HD)
        for end in range(2):
            if with_query:
                pl.when(group == end)(functools.partial(put_end, end, h, keys, values))
            else:
                put_end(end, h, keys, values)
    for source, target in zip(to_copy, end_refs):
        target[0, :, :copied] = source[0]


def project(with_query, place, q_gain, k_gain, weights, tokens, to_copy=()):
    smem = pl.BlockSpec(memory_space=pltpu.SMEM)
    vmem = pl.BlockSpec(memory_space=pltpu.VMEM)
    parts = (1, 2, 0) if with_query else (1, 2)
    count = len(tokens)
    copied = to_copy[0].shape[2] if to_copy else 0
    ends = copied + count // 4
    tiles = jax.ShapeDtypeStruct((PAIRS, count, 2, TOK, HD), BF16)
    packed = jax.ShapeDtypeStruct((PAIRS, 2, ends, 2, TOK, HD), BF16)
    tile_spec = pl.BlockSpec((1, 4, 2, TOK, HD), lambda j, g: (j, g, 0, 0, 0))

    def packed_spec(number):
        return pl.BlockSpec((1, 2, number, 2, TOK, HD), lambda j, g: (j, 0, 0, 0, 0, 0))

    return pl.pallas_call(
        functools.partial(project_kernel, with_query, copied),
        grid=(PAIRS, count // 4),
        in_specs=[smem, vmem, vmem]
        + weight_specs(parts, lambda j, g: j)
        + [pl.BlockSpec(memory_space=pl.ANY)] * count
        + [packed_spec(copied)] * len(to_copy),
        out_specs=[tile_spec] * 2 + [packed_spec(ends)] * 2 + [tile_spec] * with_query,
        out_shape=[tiles] * 2 + [packed] * 2 + [tiles] * with_query,
        scratch_shapes=[pltpu.VMEM((count, TOK, D), BF16), pltpu.SemaphoreType.DMA((count,))],
        compiler_params=pltpu.CompilerParams(vmem_limit_bytes=60 * MIB),
        cost_estimate=pl.CostEstimate(
            flops=2 * count * TOK * D * PAIRS * PAIR * len(parts),
            bytes_accessed=30 * 10**6,
            transcendentals=10**5,
        ),
        name="project",
    )(place, q_gain, k_gain, *[weights] * len(parts), *tokens, *to_copy)


def attend_kernel(edges, place_ref, radii_ref, q_ref, *refs):
    (middle, beside, diagonal), ends = (refs[0:2], refs[2:4], refs[4:6]), refs[6:-3]
    send_ref, keep_ref, sides = refs[-3:]
    core, row, col, x_lo = (place_ref[i] for i in range(4))
    pair = pl.program_id(0)
    factor = math.log2(math.e) / math.sqrt(HD)

    for which in range(2):
        for at, source in ((1 - x_lo, beside), (x_lo, diagonal)):
            sides[which, at, 1:5] = source[which][0]
        for r, above_or_below in ((0, ends[0::2]), (5, ends[1::2])):
            for at, source in zip((1 - x_lo, x_lo), above_or_below):
                sides[which, at, r] = source[0, which, source.shape[2] - 1]

    def tile_of(which, r, c, h):
        if c in (0, 3):
            return sides[which, c // 3, r, h]
        if 1 <= r <= 4:
            return middle[which][0, 2 * (r - 1) + c - 1, h]
        return ends[0 if r == 0 else 1][0, which, c - 1, h]

    def row_of(which, r, h, cols):
        return jnp.concatenate([tile_of(which, r, c, h) for c in cols], axis=0)

    def scores_of(r, h, reach_r, reach_c):
        q = jnp.concatenate([q_ref[0, 2 * (r - 1) + i, h] for i in range(2)], axis=0)
        rows, cols = range(r - reach_r, r + reach_r + 1), range(1 - reach_c, 3 + reach_c)
        return [
            lax.dot_general(
                q,
                row_of(0, at, h, cols),
                (((1,), (1,)), ((), ())),
                preferred_element_type=F32,
            )
            for at in rows
        ]

    def weights_of(scores, r, reach_r, reach_c):
        rows, cols = range(r - reach_r, r + reach_r + 1), range(1 - reach_c, 3 + reach_c)
        probs, dens = [], []
        for i in range(2):
            shown, top = [], None
            for j, at in enumerate(rows):
                for c in range(1 + i - reach_c, 2 + i + reach_c):
                    n = c - cols[0]
                    block = scores[j][i * TOK : (i + 1) * TOK, n * TOK : (n + 1) * TOK]
                    tile_r, tile_c = row * 4 + at - 1, col * 2 + c - 1
                    inside = (
                        (tile_r >= 0)
                        & (tile_r < 4 * ROWS_OF_CHIPS)
                        & (tile_c >= 0)
                        & (tile_c < 2 * COLS_OF_CHIPS)
                    )
                    offset = jnp.where(inside, 0.0, 1e30).astype(F32)
                    shown.append((j, n, block, offset))
                    if 1 <= at <= 4 and c in (1, 2):
                        seen = block
                    else:
                        seen = block - offset
                    top = seen if top is None else jnp.maximum(top, seen)
            peak = jnp.max(top, axis=-1, keepdims=True) * factor
            total = None
            prob = [[jnp.zeros((TOK, TOK), BF16)] * len(cols) for _ in rows]
            for j, n, block, offset in shown:
                weight = jnp.exp2(block * factor - (peak + offset))
                total = weight if total is None else total + weight
                prob[j][n] = weight.astype(BF16)
            probs.append(prob)
            dens.append(jnp.sum(total, axis=-1, keepdims=True))
        return probs, dens

    def mixed_of(probs, dens, r, h, reach_r, reach_c):
        rows, cols = range(r - reach_r, r + reach_r + 1), range(1 - reach_c, 3 + reach_c)
        mixed = None
        for j, at in enumerate(rows):
            weights = [jnp.concatenate(probs[i][j], axis=1) for i in range(2)]
            term = jnp.dot(
                jnp.concatenate(weights, axis=0),
                row_of(1, at, h, cols),
                preferred_element_type=F32,
            )
            mixed = term if mixed is None else mixed + term
        return [(mixed[i * TOK : (i + 1) * TOK] / dens[i]).astype(BF16) for i in range(2)]

    def attend_heads(heads, reach_r, reach_c):
        reach = reach_r, reach_c
        both = [(r, h) for h in heads for r in ((1, 4) if edges else (2, 3))]
        scores = [scores_of(r, h, *reach) for r, h in both]
        weights = [weights_of(score, r, *reach) for score, (r, h) in zip(scores, both)]
        mixed = [mixed_of(*weight, r, h, *reach) for weight, (r, h) in zip(weights, both)]
        for n, h in enumerate(heads):
            low, high = mixed[2 * n : 2 * n + 2]
            of_head = slice(h * HD, (h + 1) * HD)
            for c in range(2):
                send_ref[c, :, of_head] = jnp.where(core == 0, high[c], low[c])
                keep_ref[c, :, of_head] = jnp.where(core == 0, low[c], high[c])

    first = core * HALF_HEADS + pair * 2
    wide = [(radii_ref[first + h, 0] == 1) & (radii_ref[first + h, 1] == 1) for h in range(2)]
    pl.when(wide[0] & wide[1])(functools.partial(attend_heads, (0, 1), 1, 1))

    @pl.when(~(wide[0] & wide[1]))
    def _():
        for h in range(2):
            for reach_r in (0, 1):
                for reach_c in (0, 1):
                    taken = (radii_ref[first + h, 0] == reach_r) & (
                        radii_ref[first + h, 1] == reach_c
                    )
                    pl.when(taken)(functools.partial(attend_heads, (h,), reach_r, reach_c))


def attend(edges, place, radii, arrays):
    smem = pl.BlockSpec(memory_space=pltpu.SMEM)
    shape = jax.ShapeDtypeStruct((2, TOK, HALF_HEADS * HD), BF16)
    out = pl.BlockSpec((2, TOK, PAIR), lambda j: (0, 0, j))

    def whole(array):
        return pl.BlockSpec(
            (1,) + array.shape[1:], lambda j, rank=array.ndim: (j,) + (0,) * (rank - 1)
        )

    return pl.pallas_call(
        functools.partial(attend_kernel, edges),
        grid=(PAIRS,),
        in_specs=[smem, smem] + [whole(array) for array in arrays],
        out_specs=[out, out],
        out_shape=[shape, shape],
        scratch_shapes=[pltpu.VMEM((2, 2, 6, 2, TOK, HD), BF16)],
        compiler_params=pltpu.CompilerParams(vmem_limit_bytes=60 * MIB),
        cost_estimate=pl.CostEstimate(
            flops=7 * 10**9, bytes_accessed=15 * 10**6, transcendentals=4 * 10**6
        ),
        name="attend",
    )(place, radii, *arrays)


def assemble_kernel(place_ref, keep_ref, got_ref, *refs):
    first = place_ref[0] == 0
    out_ref = refs[-1]
    width = HALF_HEADS * HD

    def rows(ref):
        halves = [ref[c, 0].astype(F32).reshape(8, 8, width) for c in range(2)]
        return jnp.concatenate(halves, axis=1)

    mine, got = rows(keep_ref), rows(got_ref)
    out_ref[0, :, :, :width] = jnp.where(first, mine, got).astype(BF16)
    out_ref[0, :, :, width:] = jnp.where(first, got, mine).astype(BF16)


def assemble(core, tile_row, keep, got, into=None):
    width = HALF_HEADS * HD
    tiles = pl.BlockSpec((2, 1, 64, width), lambda f, t: (0, f, 0, 0))
    others = () if into is None else (into,)
    return pl.pallas_call(
        assemble_kernel,
        grid_spec=pltpu.PrefetchScalarGridSpec(
            num_scalar_prefetch=1,
            grid=(2,),
            in_specs=[tiles, tiles] + [pl.BlockSpec(memory_space=pl.ANY)] * len(others),
            out_specs=pl.BlockSpec((1, 8, 16, 2 * width), lambda f, t: (f, t[1], 0, 0)),
        ),
        out_shape=jax.ShapeDtypeStruct((2, 16, 16, 2 * width), BF16),
        input_output_aliases={3: 0} if others else {},
        name="assemble",
    )(
        jnp.stack([core, tile_row]).astype(jnp.int32),
        *[a.reshape(2, 2, 64, width) for a in (keep, got)],
        *others,
    )


def local(latents, cond_mask, radii, cond_embed, mod_shift, mod_scale, w_qkv, q_gain, k_gain):
    ha, wa = lax.axis_index("ha"), lax.axis_index("wa")
    core, row = ha % 2, ha // 2
    x_hi, x_lo = row // NZ, wa % NX_LO
    place = jnp.stack([core, row, wa, x_lo]).astype(jnp.int32)
    gains = q_gain.reshape(1, HD), k_gain.reshape(1, HD)

    def swap(*arrays):
        return tuple(send(a, swap_core) for a in arrays)

    norm_args = (x_lo, latents, cond_mask.astype(F32)[..., None], cond_embed, mod_shift, mod_scale)
    block = x_block(w_qkv, core, x_lo, x_hi)
    weights = gather_weights(block)
    edges, inners = normalize(core, *norm_args), normalize(1 - core, *norm_args)
    middle = edges + swap(*edges) + inners + swap(*inners)

    edge_near, inner_near = held_back((edges[0], inners[0]), block, *middle)
    beside = send(edge_near, swap_beside), send(inner_near, swap_beside)
    edge_far, inner_far = held_back((edges[1], inners[1]), weights)
    diagonal = send(edge_far, swap_diagonal), send(inner_far, swap_diagonal)

    def with_other(edge, inner):
        return (edge, *swap(edge), inner, *swap(inner))

    def exchange_rows(up, down):
        return send(down, next_row(1)), send(up, next_row(-1))

    key, value, up, down, query = project(True, place, *gains, weights, middle)
    *beside, up, down = project(
        False, place, *gains, weights, with_other(*beside), (up, down)
    )
    ends = exchange_rows(up, down)
    diagonal = held_back(diagonal, *beside)
    *diagonal, up, down = project(False, place, *gains, weights, with_other(*diagonal))
    ends += exchange_rows(up, down)
    arrays = (query, key, value, *beside, *diagonal)
    inner_away, inner_keep = attend(False, place, radii, arrays)
    (inner_got,) = swap(inner_away)
    out = assemble(core, 1 - core, inner_keep, inner_got)
    edge_away, edge_keep = attend(True, place, radii, arrays + ends)
    (edge_got,) = swap(edge_away)
    return assemble(core, core, edge_keep, edge_got, out)


def solution(mesh):
    in_specs = (
        P(None, "ha", "wa", None),
        P(None, "ha", "wa"),
        P(),
        P(),
        P(),
        P(),
        P(("ha", "wa"), None),
        P(),
        P(),
    )
    out_specs = P(None, "ha", "wa", None)
    return jax.shard_map(local, mesh=mesh, in_specs=in_specs, out_specs=out_specs, check_vma=False)
```

```python
import functools
import math

import jax
import jax.numpy as jnp
from jax import lax
from jax.experimental import pallas as pl
from jax.experimental.pallas import tpu as pltpu
from jax.sharding import PartitionSpec as P

AXES = ("ha", "wa")
NX_HI, NZ, NY, NX_LO = 2, 4, 4, 2
ROWS_OF_CHIPS, COLS_OF_CHIPS = NX_HI * NZ, NY * NX_LO
F32, BF16 = jnp.float32, jnp.bfloat16
D, HD, TOK = 3072, 128, 128
HALF_HEADS, PAIRS = 6, 3
PAIR = 2 * HD
MIB = 1024 * 1024


def index_of(x_hi, z, core, y, x_lo):
    return ((x_hi * NZ + z) * 2 + core) * COLS_OF_CHIPS + y * NX_LO + x_lo


def permutation(move):
    pairs = []
    for x_hi in range(NX_HI):
        for z in range(NZ):
            for core in range(2):
                for y in range(NY):
                    for x_lo in range(NX_LO):
                        target = move(x_hi, z, core, y, x_lo)
                        if target is not None:
                            pairs.append((index_of(x_hi, z, core, y, x_lo), index_of(*target)))
    return pairs


def swap_core(x_hi, z, core, y, x_lo):
    return x_hi, z, 1 - core, y, x_lo


def flip_x(bits):
    return lambda x_hi, z, core, y, x_lo: (x_hi ^ (bits >> 1), z, core, y, x_lo ^ (bits & 1))


def swap_beside(x_hi, z, core, y, x_lo):
    return x_hi, z, core, y, 1 - x_lo


def swap_diagonal(x_hi, z, core, y, x_lo):
    wa = y * NX_LO + x_lo + (1 if x_lo else -1)
    if not 0 <= wa < COLS_OF_CHIPS:
        return None
    return x_hi, z, core, wa // NX_LO, wa % NX_LO


def next_row(by):
    def move(x_hi, z, core, y, x_lo):
        q = x_hi * NZ + z + by
        if not 0 <= q < ROWS_OF_CHIPS:
            return None
        return q // NZ, q % NZ, core, y, x_lo

    return move


def send(array, move):
    return lax.ppermute(array, AXES, permutation(move))


def norm_kernel(place_ref, lat_ref, mask_ref, embed_ref, shift_ref, scale_ref, near_ref, far_ref):
    cond = lat_ref[0].astype(F32) + mask_ref[0] * embed_ref[...]
    center = cond - jnp.mean(cond, axis=-1, keepdims=True)
    spread = jnp.mean(center * center, axis=-1, keepdims=True)
    normed = center * lax.rsqrt(spread + 1e-06) * (1.0 + scale_ref[...]) + shift_ref[...]
    left, right = normed[:, :8].reshape(64, D), normed[:, 8:].reshape(64, D)
    first = place_ref[3] == 0
    near_ref[0] = jnp.where(first, right, left).astype(BF16)
    far_ref[0] = jnp.where(first, left, right).astype(BF16)


def normalize(edge, place, latents, mask, cond_embed, mod_shift, mod_scale):
    vector = pl.BlockSpec((1, 1, D), lambda f, t: (0, 0, 0))
    tile = pl.BlockSpec((1, 64, D), lambda f, t: (f, 0, 0))
    shape = jax.ShapeDtypeStruct((2, 64, D), BF16)
    left, right = pl.pallas_call(
        norm_kernel,
        grid_spec=pltpu.PrefetchScalarGridSpec(
            num_scalar_prefetch=1,
            grid=(2,),
            in_specs=[
                pl.BlockSpec((1, 8, 16, D), lambda f, t: (f, t[0] if edge else 1 - t[0], 0, 0)),
                pl.BlockSpec((1, 8, 16, 1), lambda f, t: (f, t[0] if edge else 1 - t[0], 0, 0)),
                vector,
                vector,
                vector,
            ],
            out_specs=[tile, tile],
        ),
        out_shape=[shape, shape],
        compiler_params=pltpu.CompilerParams(vmem_limit_bytes=48 * MIB),
        name="norm",
    )(
        place,
        latents,
        mask,
        cond_embed.reshape(1, 1, D),
        mod_shift.reshape(1, 1, D),
        mod_scale.reshape(1, 1, D),
    )
    return left.reshape(TOK, D), right.reshape(TOK, D)


def x_block(w_qkv, core, x_lo, x_hi):
    rows = w_qkv.shape[0]
    split = w_qkv.reshape(rows, 3, 2, HALF_HEADS * HD)
    first, second = split[:, :, 0], split[:, :, 1]
    mine = jnp.where(core == 0, first, second)
    theirs = jnp.where(core == 0, second, first)
    got = send(theirs, swap_core)
    both = jnp.where(core == 0, jnp.stack([mine, got]), jnp.stack([got, mine]))
    flips = [both] + [send(both, flip_x(bits)) for bits in (1, 2, 3)]

    def pair(same, other):
        return jnp.where(
            x_lo == 0,
            jnp.concatenate([same, other], axis=1),
            jnp.concatenate([other, same], axis=1),
        )

    here, there = pair(flips[0], flips[1]), pair(flips[2], flips[3])
    return jnp.where(x_hi == 0, jnp.stack([here, there]), jnp.stack([there, here]))


def yz_groups():
    return [
        [index_of(x_hi, z, core, y, x_lo) for z in range(NZ) for y in range(NY)]
        for x_hi in range(NX_HI)
        for core in range(2)
        for x_lo in range(NX_LO)
    ]


def gather_weights(block):
    shape = block.shape[:3] + (3 * HALF_HEADS * HD,)
    whole = lax.all_gather(
        block.reshape(-1, shape[-1]), AXES, axis=0, tiled=True, axis_index_groups=yz_groups()
    )
    return whole.reshape(NZ * NY, *shape)


def held_back(arrays, *others):
    return lax.optimization_barrier((tuple(arrays), others))[0]


def columns(w_ref):
    blocks = [
        w_ref[z * NY + y, x_hi, core]
        for x_hi in range(NX_HI)
        for z in range(NZ)
        for core in range(2)
        for y in range(NY)
    ]
    return jnp.concatenate(blocks, axis=0)


def head_norm(block, gain_ref):
    square = jnp.mean(block * block, axis=-1, keepdims=True)
    return (block * lax.rsqrt(square + 1e-06) * gain_ref[...]).astype(BF16)


def weight_specs(parts, index):
    return [
        pl.BlockSpec(
            (NZ * NY, NX_HI, 2, 48, PAIR),
            lambda *ids, part=part: (0, 0, 0, 0, part * PAIRS + index(*ids)),
        )
        for part in parts
    ]


def project_kernel(with_query, copied, place_ref, q_gain_ref, k_gain_ref, *refs):
    groups = 2 if with_query else 1
    weights, refs = refs[: 2 + with_query], refs[2 + with_query :]
    tokens, refs = refs[: 4 * groups], refs[4 * groups :]
    to_copy, refs = refs[: 2 if copied else 0], refs[2 if copied else 0 :]
    k_ref, v_ref, *end_refs = refs[:4]
    q_ref = refs[4] if with_query else None
    xs, x_sem = refs[-2:]
    core, x_lo = place_ref[0], place_ref[3]
    pair, group = pl.program_id(0), pl.program_id(1)
    width = 2 if with_query else 1

    @pl.when((pair == 0) & (group == 0))
    def _():
        rows = (3 * core, 3 - 3 * core, 1 + core, 2 - core)
        for t, source in enumerate(tokens):
            at = rows[t // width] * width
            if with_query:
                at += 1 - x_lo if t % 2 == 0 else x_lo
            pltpu.make_async_copy(source, xs.at[at], x_sem.at[at]).start()

    @pl.when(pair == 0)
    def _():
        for t in range(4):
            at = group * 4 + t
            pltpu.make_async_copy(xs.at[at], xs.at[at], x_sem.at[at]).wait()

    def project(w_ref):
        x = xs[pl.ds(group * 4, 4)].reshape(4 * TOK, D)
        return jnp.dot(x, columns(w_ref), preferred_element_type=F32)

    def put_end(end, h, keys, values):
        at = 3 * end if width == 1 else 2 * end
        end_refs[end][0, 0, copied:, h] = keys[at : at + width]
        end_refs[end][0, 1, copied:, h] = values[at : at + width]

    key, value = project(weights[0]), project(weights[1])
    query = project(weights[2]) if with_query else None
    for h in range(2):
        of_head = slice(h * HD, (h + 1) * HD)
        keys = head_norm(key[:, of_head], k_gain_ref).reshape(4, TOK, HD)
        values = value[:, of_head].astype(BF16).reshape(4, TOK, HD)
        k_ref[0, :, h] = keys
        v_ref[0, :, h] = values
        if with_query:
            q_ref[0, :, h] = head_norm(query[:, of_head], q_gain_ref).reshape(4, TOK, HD)
        for end in range(2):
            if with_query:
                pl.when(group == end)(functools.partial(put_end, end, h, keys, values))
            else:
                put_end(end, h, keys, values)
    for source, target in zip(to_copy, end_refs):
        target[0, :, :copied] = source[0]


def project(with_query, place, q_gain, k_gain, weights, tokens, to_copy=()):
    smem = pl.BlockSpec(memory_space=pltpu.SMEM)
    vmem = pl.BlockSpec(memory_space=pltpu.VMEM)
    parts = (1, 2, 0) if with_query else (1, 2)
    count = len(tokens)
    copied = to_copy[0].shape[2] if to_copy else 0
    ends = copied + count // 4
    tiles = jax.ShapeDtypeStruct((PAIRS, count, 2, TOK, HD), BF16)
    packed = jax.ShapeDtypeStruct((PAIRS, 2, ends, 2, TOK, HD), BF16)
    tile_spec = pl.BlockSpec((1, 4, 2, TOK, HD), lambda j, g: (j, g, 0, 0, 0))

    def packed_spec(number):
        return pl.BlockSpec((1, 2, number, 2, TOK, HD), lambda j, g: (j, 0, 0, 0, 0, 0))

    return pl.pallas_call(
        functools.partial(project_kernel, with_query, copied),
        grid=(PAIRS, count // 4),
        in_specs=[smem, vmem, vmem]
        + weight_specs(parts, lambda j, g: j)
        + [pl.BlockSpec(memory_space=pl.ANY)] * count
        + [packed_spec(copied)] * len(to_copy),
        out_specs=[tile_spec] * 2 + [packed_spec(ends)] * 2 + [tile_spec] * with_query,
        out_shape=[tiles] * 2 + [packed] * 2 + [tiles] * with_query,
        scratch_shapes=[pltpu.VMEM((count, TOK, D), BF16), pltpu.SemaphoreType.DMA((count,))],
        compiler_params=pltpu.CompilerParams(vmem_limit_bytes=62 * MIB),
        cost_estimate=pl.CostEstimate(
            flops=2 * count * TOK * D * PAIRS * PAIR * len(parts),
            bytes_accessed=30 * 10**6,
            transcendentals=10**5,
        ),
        name="project",
    )(place, q_gain, k_gain, *[weights] * len(parts), *tokens, *to_copy)


def attend_kernel(edges, place_ref, q_ref, *refs):
    (middle, beside, diagonal), ends = (refs[0:2], refs[2:4], refs[4:6]), refs[6:-3]
    send_ref, keep_ref, sides = refs[-3:]
    core, row, col, x_lo = (place_ref[i] for i in range(4))
    pair = pl.program_id(0)
    factor = math.log2(math.e) / math.sqrt(HD)

    for which in range(2):
        for at, source in ((1 - x_lo, beside), (x_lo, diagonal)):
            sides[which, at, 1:5] = source[which][0]
        for r, above_or_below in ((0, ends[0::2]), (5, ends[1::2])):
            for at, source in zip((1 - x_lo, x_lo), above_or_below):
                sides[which, at, r] = source[0, which, source.shape[2] - 1]

    def tile_of(which, r, c, h):
        if c in (0, 3):
            return sides[which, c // 3, r, h]
        if 1 <= r <= 4:
            return middle[which][0, 2 * (r - 1) + c - 1, h]
        return ends[0 if r == 0 else 1][0, which, c - 1, h]

    def row_of(which, r, h, cols):
        return jnp.concatenate([tile_of(which, r, c, h) for c in cols], axis=0)

    def scores_of(r, h, reach_r, reach_c):
        q = jnp.concatenate([q_ref[0, 2 * (r - 1) + i, h] for i in range(2)], axis=0)
        rows, cols = range(r - reach_r, r + reach_r + 1), range(1 - reach_c, 3 + reach_c)
        return [
            lax.dot_general(
                q,
                row_of(0, at, h, cols),
                (((1,), (1,)), ((), ())),
                preferred_element_type=F32,
            )
            for at in rows
        ]

    def weights_of(scores, r, reach_r, reach_c):
        rows, cols = range(r - reach_r, r + reach_r + 1), range(1 - reach_c, 3 + reach_c)
        probs, dens = [], []
        for i in range(2):
            shown, top = [], None
            for j, at in enumerate(rows):
                for c in range(1 + i - reach_c, 2 + i + reach_c):
                    n = c - cols[0]
                    block = scores[j][i * TOK : (i + 1) * TOK, n * TOK : (n + 1) * TOK]
                    tile_r, tile_c = row * 4 + at - 1, col * 2 + c - 1
                    inside = (
                        (tile_r >= 0)
                        & (tile_r < 4 * ROWS_OF_CHIPS)
                        & (tile_c >= 0)
                        & (tile_c < 2 * COLS_OF_CHIPS)
                    )
                    offset = jnp.where(inside, 0.0, 1e30).astype(F32)
                    shown.append((j, n, block, offset))
                    if 1 <= at <= 4 and c in (1, 2):
                        seen = block
                    else:
                        seen = block - offset
                    top = seen if top is None else jnp.maximum(top, seen)
            peak = jnp.max(top, axis=-1, keepdims=True) * factor
            total = None
            prob = [[jnp.zeros((TOK, TOK), BF16)] * len(cols) for _ in rows]
            for j, n, block, offset in shown:
                weight = jnp.exp2(block * factor - (peak + offset))
                total = weight if total is None else total + weight
                prob[j][n] = weight.astype(BF16)
            probs.append(prob)
            dens.append(jnp.sum(total, axis=-1, keepdims=True))
        return probs, dens

    def mixed_of(probs, dens, r, h, reach_r, reach_c):
        rows, cols = range(r - reach_r, r + reach_r + 1), range(1 - reach_c, 3 + reach_c)
        mixed = None
        for j, at in enumerate(rows):
            weights = [jnp.concatenate(probs[i][j], axis=1) for i in range(2)]
            term = jnp.dot(
                jnp.concatenate(weights, axis=0),
                row_of(1, at, h, cols),
                preferred_element_type=F32,
            )
            mixed = term if mixed is None else mixed + term
        return [(mixed[i * TOK : (i + 1) * TOK] / dens[i]).astype(BF16) for i in range(2)]

    def attend_heads(heads, reach_r, reach_c):
        reach = reach_r, reach_c
        both = [(r, h) for h in heads for r in ((1, 4) if edges else (2, 3))]
        scores = [scores_of(r, h, *reach) for r, h in both]
        weights = [weights_of(score, r, *reach) for score, (r, h) in zip(scores, both)]
        mixed = [mixed_of(*weight, r, h, *reach) for weight, (r, h) in zip(weights, both)]
        for n, h in enumerate(heads):
            low, high = mixed[2 * n : 2 * n + 2]
            of_head = slice(h * HD, (h + 1) * HD)
            for c in range(2):
                send_ref[c, :, of_head] = jnp.where(core == 0, high[c], low[c])
                keep_ref[c, :, of_head] = jnp.where(core == 0, low[c], high[c])

    def reach(h, axis):
        return place_ref[4 + 2 * (core * HALF_HEADS + pair * 2 + h) + axis]

    wide = [(reach(h, 0) == 1) & (reach(h, 1) == 1) for h in range(2)]
    pl.when(wide[0] & wide[1])(functools.partial(attend_heads, (0, 1), 1, 1))

    @pl.when(~(wide[0] & wide[1]))
    def _():
        for h in range(2):
            for reach_r in (0, 1):
                for reach_c in (0, 1):
                    taken = (reach(h, 0) == reach_r) & (reach(h, 1) == reach_c)
                    pl.when(taken)(functools.partial(attend_heads, (h,), reach_r, reach_c))


def attend(edges, place, arrays):
    smem = pl.BlockSpec(memory_space=pltpu.SMEM)
    shape = jax.ShapeDtypeStruct((2, TOK, HALF_HEADS * HD), BF16)
    out = pl.BlockSpec((2, TOK, PAIR), lambda j: (0, 0, j))

    def whole(array):
        return pl.BlockSpec(
            (1,) + array.shape[1:], lambda j, rank=array.ndim: (j,) + (0,) * (rank - 1)
        )

    return pl.pallas_call(
        functools.partial(attend_kernel, edges),
        grid=(PAIRS,),
        in_specs=[smem] + [whole(array) for array in arrays],
        out_specs=[out, out],
        out_shape=[shape, shape],
        scratch_shapes=[pltpu.VMEM((2, 2, 6, 2, TOK, HD), BF16)],
        compiler_params=pltpu.CompilerParams(vmem_limit_bytes=62 * MIB),
        cost_estimate=pl.CostEstimate(
            flops=7 * 10**9, bytes_accessed=15 * 10**6, transcendentals=4 * 10**6
        ),
        name="attend",
    )(place, *arrays)


def assemble_kernel(place_ref, keep_ref, got_ref, *refs):
    first = place_ref[0] == 0
    out_ref = refs[-1]
    width = HALF_HEADS * HD

    def rows(ref):
        halves = [ref[c, 0].astype(F32).reshape(8, 8, width) for c in range(2)]
        return jnp.concatenate(halves, axis=1)

    mine, got = rows(keep_ref), rows(got_ref)
    out_ref[0, :, :, :width] = jnp.where(first, mine, got).astype(BF16)
    out_ref[0, :, :, width:] = jnp.where(first, got, mine).astype(BF16)


def assemble(edge, place, keep, got, into=None):
    width = HALF_HEADS * HD
    tiles = pl.BlockSpec((2, 1, 64, width), lambda f, t: (0, f, 0, 0))
    others = () if into is None else (into,)
    return pl.pallas_call(
        assemble_kernel,
        grid_spec=pltpu.PrefetchScalarGridSpec(
            num_scalar_prefetch=1,
            grid=(2,),
            in_specs=[tiles, tiles] + [pl.BlockSpec(memory_space=pl.ANY)] * len(others),
            out_specs=pl.BlockSpec(
                (1, 8, 16, 2 * width), lambda f, t: (f, t[0] if edge else 1 - t[0], 0, 0)
            ),
        ),
        out_shape=jax.ShapeDtypeStruct((2, 16, 16, 2 * width), BF16),
        compiler_params=pltpu.CompilerParams(vmem_limit_bytes=62 * MIB),
        input_output_aliases={3: 0} if others else {},
        name="assemble",
    )(
        place,
        *[a.reshape(2, 2, 64, width) for a in (keep, got)],
        *others,
    )


def local(latents, cond_mask, radii, cond_embed, mod_shift, mod_scale, w_qkv, q_gain, k_gain):
    ha, wa = lax.axis_index("ha"), lax.axis_index("wa")
    core, row = ha % 2, ha // 2
    x_hi, x_lo = row // NZ, wa % NX_LO
    place = jnp.concatenate([jnp.stack([core, row, wa, x_lo]), radii.reshape(-1)]).astype(jnp.int32)
    gains = q_gain.reshape(1, HD), k_gain.reshape(1, HD)

    def swap(*arrays):
        return tuple(send(a, swap_core) for a in arrays)

    norm_args = (place, latents, cond_mask.astype(F32)[..., None], cond_embed, mod_shift, mod_scale)
    block = x_block(w_qkv, core, x_lo, x_hi)
    weights = gather_weights(block)
    edges, inners = normalize(True, *norm_args), normalize(False, *norm_args)
    middle = edges + swap(*edges) + inners + swap(*inners)

    edge_near, inner_near = held_back((edges[0], inners[0]), block, *middle)
    beside = send(edge_near, swap_beside), send(inner_near, swap_beside)
    edge_far, inner_far = held_back((edges[1], inners[1]), weights)
    diagonal = send(edge_far, swap_diagonal), send(inner_far, swap_diagonal)

    def with_other(edge, inner):
        return (edge, *swap(edge), inner, *swap(inner))

    def exchange_rows(up, down):
        return send(down, next_row(1)), send(up, next_row(-1))

    key, value, up, down, query = project(True, place, *gains, weights, middle)
    *beside, up, down = project(
        False, place, *gains, weights, with_other(*beside), (up, down)
    )
    ends = exchange_rows(up, down)
    diagonal = held_back(diagonal, *beside)
    *diagonal, up, down = project(False, place, *gains, weights, with_other(*diagonal))
    ends += exchange_rows(up, down)
    arrays = (query, key, value, *beside, *diagonal)
    inner_away, inner_keep = attend(False, place, arrays)
    (inner_got,) = swap(inner_away)
    out = assemble(False, place, inner_keep, inner_got)
    edge_away, edge_keep = attend(True, place, arrays + ends)
    (edge_got,) = swap(edge_away)
    return assemble(True, place, edge_keep, edge_got, out)


def solution(mesh):
    in_specs = (
        P(None, "ha", "wa", None),
        P(None, "ha", "wa"),
        P(),
        P(),
        P(),
        P(),
        P(("ha", "wa"), None),
        P(),
        P(),
    )
    out_specs = P(None, "ha", "wa", None)
    return jax.shard_map(local, mesh=mesh, in_specs=in_specs, out_specs=out_specs, check_vma=False)
```

```python
import functools
import math

import jax
import jax.numpy as jnp
from jax import lax
from jax.experimental import pallas as pl
from jax.experimental.pallas import tpu as pltpu
from jax.sharding import PartitionSpec as P

AXES = ("ha", "wa")
NX_HI, NZ, NY, NX_LO = 2, 4, 4, 2
ROWS_OF_CHIPS, COLS_OF_CHIPS = NX_HI * NZ, NY * NX_LO
F32, BF16 = jnp.float32, jnp.bfloat16
D, HD, TOK = 3072, 128, 128
HALF_HEADS, PAIRS = 6, 3
PAIR = 2 * HD
MIB = 1024 * 1024


def index_of(x_hi, z, core, y, x_lo):
    return ((x_hi * NZ + z) * 2 + core) * COLS_OF_CHIPS + y * NX_LO + x_lo


def permutation(move):
    pairs = []
    for x_hi in range(NX_HI):
        for z in range(NZ):
            for core in range(2):
                for y in range(NY):
                    for x_lo in range(NX_LO):
                        target = move(x_hi, z, core, y, x_lo)
                        if target is not None:
                            pairs.append((index_of(x_hi, z, core, y, x_lo), index_of(*target)))
    return pairs


def swap_core(x_hi, z, core, y, x_lo):
    return x_hi, z, 1 - core, y, x_lo


def flip_x(bits):
    return lambda x_hi, z, core, y, x_lo: (x_hi ^ (bits >> 1), z, core, y, x_lo ^ (bits & 1))


def swap_beside(x_hi, z, core, y, x_lo):
    return x_hi, z, core, y, 1 - x_lo


def swap_diagonal(x_hi, z, core, y, x_lo):
    wa = y * NX_LO + x_lo + (1 if x_lo else -1)
    if not 0 <= wa < COLS_OF_CHIPS:
        return None
    return x_hi, z, core, wa // NX_LO, wa % NX_LO


def next_row(by):
    def move(x_hi, z, core, y, x_lo):
        q = x_hi * NZ + z + by
        if not 0 <= q < ROWS_OF_CHIPS:
            return None
        return q // NZ, q % NZ, core, y, x_lo

    return move


def send(array, move):
    return lax.ppermute(array, AXES, permutation(move))


def norm_kernel(place_ref, lat_ref, mask_ref, embed_ref, shift_ref, scale_ref, near_ref, far_ref):
    cond = lat_ref[0].astype(F32) + mask_ref[0] * embed_ref[...]
    center = cond - jnp.mean(cond, axis=-1, keepdims=True)
    spread = jnp.mean(center * center, axis=-1, keepdims=True)
    normed = center * lax.rsqrt(spread + 1e-06) * (1.0 + scale_ref[...]) + shift_ref[...]
    left, right = normed[:, :8].reshape(64, D), normed[:, 8:].reshape(64, D)
    first = place_ref[3] == 0
    near_ref[0] = jnp.where(first, right, left).astype(BF16)
    far_ref[0] = jnp.where(first, left, right).astype(BF16)


def normalize(edge, place, latents, mask, cond_embed, mod_shift, mod_scale):
    vector = pl.BlockSpec((1, 1, D), lambda f, t: (0, 0, 0))
    tile = pl.BlockSpec((1, 64, D), lambda f, t: (f, 0, 0))
    shape = jax.ShapeDtypeStruct((2, 64, D), BF16)
    left, right = pl.pallas_call(
        norm_kernel,
        grid_spec=pltpu.PrefetchScalarGridSpec(
            num_scalar_prefetch=1,
            grid=(2,),
            in_specs=[
                pl.BlockSpec((1, 8, 16, D), lambda f, t: (f, t[0] if edge else 1 - t[0], 0, 0)),
                pl.BlockSpec((1, 8, 16, 1), lambda f, t: (f, t[0] if edge else 1 - t[0], 0, 0)),
                vector,
                vector,
                vector,
            ],
            out_specs=[tile, tile],
        ),
        out_shape=[shape, shape],
        compiler_params=pltpu.CompilerParams(vmem_limit_bytes=48 * MIB),
        name="norm",
    )(
        place,
        latents,
        mask,
        cond_embed.reshape(1, 1, D),
        mod_shift.reshape(1, 1, D),
        mod_scale.reshape(1, 1, D),
    )
    return left.reshape(TOK, D), right.reshape(TOK, D)


def x_block(w_qkv, core, x_lo, x_hi):
    width = HALF_HEADS * HD

    def half(number):
        starts = [(2 * part + number) * width for part in range(3)]
        return jnp.concatenate([w_qkv[:, start : start + width] for start in starts], axis=1)

    first, second = half(0), half(1)
    mine = jnp.where(core == 0, first, second)
    theirs = jnp.where(core == 0, second, first)
    got = send(theirs, swap_core)
    both = jnp.where(core == 0, jnp.stack([mine, got]), jnp.stack([got, mine]))
    flips = [both] + [send(both, flip_x(bits)) for bits in (1, 2, 3)]

    def pair(same, other):
        return jnp.where(
            x_lo == 0,
            jnp.concatenate([same, other], axis=1),
            jnp.concatenate([other, same], axis=1),
        )

    here, there = pair(flips[0], flips[1]), pair(flips[2], flips[3])
    return jnp.where(x_hi == 0, jnp.stack([here, there]), jnp.stack([there, here]))


def yz_groups():
    return [
        [index_of(x_hi, z, core, y, x_lo) for z in range(NZ) for y in range(NY)]
        for x_hi in range(NX_HI)
        for core in range(2)
        for x_lo in range(NX_LO)
    ]


def gather_weights(block):
    whole = lax.all_gather(
        block.reshape(-1, block.shape[-1]),
        AXES,
        axis=0,
        tiled=True,
        axis_index_groups=yz_groups(),
    )
    return whole.reshape(NZ * NY, *block.shape)


def held_back(arrays, *others):
    return lax.optimization_barrier((tuple(arrays), others))[0]


def columns(w_ref):
    blocks = [
        w_ref[z * NY + y, x_hi, core]
        for x_hi in range(NX_HI)
        for z in range(NZ)
        for core in range(2)
        for y in range(NY)
    ]
    return jnp.concatenate(blocks, axis=0)


def head_norm(block, gain_ref):
    square = jnp.mean(block * block, axis=-1, keepdims=True)
    return (block * lax.rsqrt(square + 1e-06) * gain_ref[...]).astype(BF16)


def weight_specs(parts, index):
    return [
        pl.BlockSpec(
            (NZ * NY, NX_HI, 2, 48, PAIR),
            lambda *ids, part=part: (0, 0, 0, 0, part * PAIRS + index(*ids)),
        )
        for part in parts
    ]


def project_kernel(with_query, copied, place_ref, q_gain_ref, k_gain_ref, *refs):
    groups = 2 if with_query else 1
    weights, refs = refs[: 2 + with_query], refs[2 + with_query :]
    tokens, refs = refs[: 4 * groups], refs[4 * groups :]
    to_copy, refs = refs[: 2 if copied else 0], refs[2 if copied else 0 :]
    k_ref, v_ref, *end_refs = refs[:4]
    q_ref = refs[4] if with_query else None
    xs, x_sem = refs[-2:]
    core, x_lo = place_ref[0], place_ref[3]
    pair, group = pl.program_id(0), pl.program_id(1)
    width = 2 if with_query else 1

    @pl.when((pair == 0) & (group == 0))
    def _():
        rows = (3 * core, 3 - 3 * core, 1 + core, 2 - core)
        for t, source in enumerate(tokens):
            at = rows[t // width] * width
            if with_query:
                at += 1 - x_lo if t % 2 == 0 else x_lo
            pltpu.make_async_copy(source, xs.at[at], x_sem.at[at]).start()

    @pl.when(pair == 0)
    def _():
        for t in range(4):
            at = group * 4 + t
            pltpu.make_async_copy(xs.at[at], xs.at[at], x_sem.at[at]).wait()

    def project(w_ref):
        x = xs[pl.ds(group * 4, 4)].reshape(4 * TOK, D)
        return jnp.dot(x, columns(w_ref), preferred_element_type=F32)

    def put_end(end, h, keys, values):
        at = 3 * end if width == 1 else 2 * end
        end_refs[end][0, 0, copied:, h] = keys[at : at + width]
        end_refs[end][0, 1, copied:, h] = values[at : at + width]

    key, value = project(weights[0]), project(weights[1])
    query = project(weights[2]) if with_query else None
    for h in range(2):
        of_head = slice(h * HD, (h + 1) * HD)
        keys = head_norm(key[:, of_head], k_gain_ref).reshape(4, TOK, HD)
        values = value[:, of_head].astype(BF16).reshape(4, TOK, HD)
        k_ref[0, :, h] = keys
        v_ref[0, :, h] = values
        if with_query:
            q_ref[0, :, h] = head_norm(query[:, of_head], q_gain_ref).reshape(4, TOK, HD)
        for end in range(2):
            if with_query:
                pl.when(group == end)(functools.partial(put_end, end, h, keys, values))
            else:
                put_end(end, h, keys, values)
    for source, target in zip(to_copy, end_refs):
        target[0, :, :copied] = source[0]


def project(with_query, place, q_gain, k_gain, weights, tokens, to_copy=()):
    smem = pl.BlockSpec(memory_space=pltpu.SMEM)
    vmem = pl.BlockSpec(memory_space=pltpu.VMEM)
    parts = (1, 2, 0) if with_query else (1, 2)
    count = len(tokens)
    copied = to_copy[0].shape[2] if to_copy else 0
    ends = copied + count // 4
    tiles = jax.ShapeDtypeStruct((PAIRS, count, 2, TOK, HD), BF16)
    packed = jax.ShapeDtypeStruct((PAIRS, 2, ends, 2, TOK, HD), BF16)
    tile_spec = pl.BlockSpec((1, 4, 2, TOK, HD), lambda j, g: (j, g, 0, 0, 0))

    def packed_spec(number):
        return pl.BlockSpec((1, 2, number, 2, TOK, HD), lambda j, g: (j, 0, 0, 0, 0, 0))

    return pl.pallas_call(
        functools.partial(project_kernel, with_query, copied),
        grid=(PAIRS, count // 4),
        in_specs=[smem, vmem, vmem]
        + weight_specs(parts, lambda j, g: j)
        + [pl.BlockSpec(memory_space=pl.ANY)] * count
        + [packed_spec(copied)] * len(to_copy),
        out_specs=[tile_spec] * 2 + [packed_spec(ends)] * 2 + [tile_spec] * with_query,
        out_shape=[tiles] * 2 + [packed] * 2 + [tiles] * with_query,
        scratch_shapes=[pltpu.VMEM((count, TOK, D), BF16), pltpu.SemaphoreType.DMA((count,))],
        compiler_params=pltpu.CompilerParams(vmem_limit_bytes=62 * MIB),
        cost_estimate=pl.CostEstimate(
            flops=2 * count * TOK * D * PAIRS * PAIR * len(parts),
            bytes_accessed=30 * 10**6,
            transcendentals=10**5,
        ),
        name="project",
    )(place, q_gain, k_gain, *[weights] * len(parts), *tokens, *to_copy)


def attend_kernel(edges, place_ref, q_ref, *refs):
    (middle, beside, diagonal), ends = (refs[0:2], refs[2:4], refs[4:6]), refs[6:-3]
    send_ref, keep_ref, sides = refs[-3:]
    core, row, col, x_lo = (place_ref[i] for i in range(4))
    pair = pl.program_id(0)
    factor = math.log2(math.e) / math.sqrt(HD)

    for which in range(2):
        for at, source in ((1 - x_lo, beside), (x_lo, diagonal)):
            sides[which, at, 1:5] = source[which][0]
        for r, above_or_below in ((0, ends[0::2]), (5, ends[1::2])):
            for at, source in zip((1 - x_lo, x_lo), above_or_below):
                sides[which, at, r] = source[0, which, source.shape[2] - 1]

    def tile_of(which, r, c, h):
        if c in (0, 3):
            return sides[which, c // 3, r, h]
        if 1 <= r <= 4:
            return middle[which][0, 2 * (r - 1) + c - 1, h]
        return ends[0 if r == 0 else 1][0, which, c - 1, h]

    def row_of(which, r, h, cols):
        return jnp.concatenate([tile_of(which, r, c, h) for c in cols], axis=0)

    def scores_of(r, h, reach_r, reach_c):
        q = jnp.concatenate([q_ref[0, 2 * (r - 1) + i, h] for i in range(2)], axis=0)
        rows, cols = range(r - reach_r, r + reach_r + 1), range(1 - reach_c, 3 + reach_c)
        return [
            lax.dot_general(
                q,
                row_of(0, at, h, cols),
                (((1,), (1,)), ((), ())),
                preferred_element_type=F32,
            )
            for at in rows
        ]

    def weights_of(scores, r, reach_r, reach_c):
        rows, cols = range(r - reach_r, r + reach_r + 1), range(1 - reach_c, 3 + reach_c)
        probs, dens = [], []
        for i in range(2):
            shown, top = [], None
            for j, at in enumerate(rows):
                for c in range(1 + i - reach_c, 2 + i + reach_c):
                    n = c - cols[0]
                    block = scores[j][i * TOK : (i + 1) * TOK, n * TOK : (n + 1) * TOK]
                    tile_r, tile_c = row * 4 + at - 1, col * 2 + c - 1
                    inside = (
                        (tile_r >= 0)
                        & (tile_r < 4 * ROWS_OF_CHIPS)
                        & (tile_c >= 0)
                        & (tile_c < 2 * COLS_OF_CHIPS)
                    )
                    offset = jnp.where(inside, 0.0, 1e30).astype(F32)
                    shown.append((j, n, block, offset))
                    if 1 <= at <= 4 and c in (1, 2):
                        seen = block
                    else:
                        seen = block - offset
                    top = seen if top is None else jnp.maximum(top, seen)
            peak = jnp.max(top, axis=-1, keepdims=True) * factor
            total = None
            prob = [[jnp.zeros((TOK, TOK), BF16)] * len(cols) for _ in rows]
            for j, n, block, offset in shown:
                weight = jnp.exp2(block * factor - (peak + offset))
                total = weight if total is None else total + weight
                prob[j][n] = weight.astype(BF16)
            probs.append(prob)
            dens.append(jnp.sum(total, axis=-1, keepdims=True))
        return probs, dens

    def mixed_of(probs, dens, r, h, reach_r, reach_c):
        rows, cols = range(r - reach_r, r + reach_r + 1), range(1 - reach_c, 3 + reach_c)
        mixed = None
        for j, at in enumerate(rows):
            weights = [jnp.concatenate(probs[i][j], axis=1) for i in range(2)]
            term = jnp.dot(
                jnp.concatenate(weights, axis=0),
                row_of(1, at, h, cols),
                preferred_element_type=F32,
            )
            mixed = term if mixed is None else mixed + term
        return [(mixed[i * TOK : (i + 1) * TOK] / dens[i]).astype(BF16) for i in range(2)]

    def attend_heads(heads, reach_r, reach_c):
        reach = reach_r, reach_c
        both = [(r, h) for h in heads for r in ((1, 4) if edges else (2, 3))]
        scores = [scores_of(r, h, *reach) for r, h in both]
        weights = [weights_of(score, r, *reach) for score, (r, h) in zip(scores, both)]
        mixed = [mixed_of(*weight, r, h, *reach) for weight, (r, h) in zip(weights, both)]
        for n, h in enumerate(heads):
            low, high = mixed[2 * n : 2 * n + 2]
            of_head = slice(h * HD, (h + 1) * HD)
            for c in range(2):
                send_ref[c, :, of_head] = jnp.where(core == 0, high[c], low[c])
                keep_ref[c, :, of_head] = jnp.where(core == 0, low[c], high[c])

    def reach(h, axis):
        return place_ref[4 + 2 * (core * HALF_HEADS + pair * 2 + h) + axis]

    wide = [(reach(h, 0) == 1) & (reach(h, 1) == 1) for h in range(2)]
    pl.when(wide[0] & wide[1])(functools.partial(attend_heads, (0, 1), 1, 1))

    @pl.when(~(wide[0] & wide[1]))
    def _():
        for h in range(2):
            for reach_r in (0, 1):
                for reach_c in (0, 1):
                    taken = (reach(h, 0) == reach_r) & (reach(h, 1) == reach_c)
                    pl.when(taken)(functools.partial(attend_heads, (h,), reach_r, reach_c))


def attend(edges, place, arrays):
    smem = pl.BlockSpec(memory_space=pltpu.SMEM)
    shape = jax.ShapeDtypeStruct((2, TOK, HALF_HEADS * HD), BF16)
    out = pl.BlockSpec((2, TOK, PAIR), lambda j: (0, 0, j))

    def whole(array):
        return pl.BlockSpec(
            (1,) + array.shape[1:], lambda j, rank=array.ndim: (j,) + (0,) * (rank - 1)
        )

    return pl.pallas_call(
        functools.partial(attend_kernel, edges),
        grid=(PAIRS,),
        in_specs=[smem] + [whole(array) for array in arrays],
        out_specs=[out, out],
        out_shape=[shape, shape],
        scratch_shapes=[pltpu.VMEM((2, 2, 6, 2, TOK, HD), BF16)],
        compiler_params=pltpu.CompilerParams(vmem_limit_bytes=62 * MIB),
        cost_estimate=pl.CostEstimate(
            flops=7 * 10**9, bytes_accessed=15 * 10**6, transcendentals=4 * 10**6
        ),
        name="attend",
    )(place, *arrays)


def assemble_kernel(place_ref, keep_ref, got_ref, *refs):
    first = place_ref[0] == 0
    out_ref = refs[-1]
    width = HALF_HEADS * HD

    def rows(ref):
        halves = [ref[c, 0].astype(F32).reshape(8, 8, width) for c in range(2)]
        return jnp.concatenate(halves, axis=1)

    mine, got = rows(keep_ref), rows(got_ref)
    out_ref[0, :, :, :width] = jnp.where(first, mine, got).astype(BF16)
    out_ref[0, :, :, width:] = jnp.where(first, got, mine).astype(BF16)


def assemble(edge, place, keep, got, into=None):
    width = HALF_HEADS * HD
    tiles = pl.BlockSpec((2, 1, 64, width), lambda f, t: (0, f, 0, 0))
    others = () if into is None else (into,)
    return pl.pallas_call(
        assemble_kernel,
        grid_spec=pltpu.PrefetchScalarGridSpec(
            num_scalar_prefetch=1,
            grid=(2,),
            in_specs=[tiles, tiles] + [pl.BlockSpec(memory_space=pl.ANY)] * len(others),
            out_specs=pl.BlockSpec(
                (1, 8, 16, 2 * width), lambda f, t: (f, t[0] if edge else 1 - t[0], 0, 0)
            ),
        ),
        out_shape=jax.ShapeDtypeStruct((2, 16, 16, 2 * width), BF16),
        compiler_params=pltpu.CompilerParams(vmem_limit_bytes=62 * MIB),
        input_output_aliases={3: 0} if others else {},
        name="assemble",
    )(
        place,
        *[a.reshape(2, 2, 64, width) for a in (keep, got)],
        *others,
    )


def local(latents, cond_mask, radii, cond_embed, mod_shift, mod_scale, w_qkv, q_gain, k_gain):
    ha, wa = lax.axis_index("ha"), lax.axis_index("wa")
    core, row = ha % 2, ha // 2
    x_hi, x_lo = row // NZ, wa % NX_LO
    place = jnp.concatenate([jnp.stack([core, row, wa, x_lo]), radii.reshape(-1)]).astype(jnp.int32)
    gains = q_gain.reshape(1, HD), k_gain.reshape(1, HD)

    def swap(*arrays):
        return tuple(send(a, swap_core) for a in arrays)

    norm_args = (place, latents, cond_mask.astype(F32)[..., None], cond_embed, mod_shift, mod_scale)
    block = x_block(w_qkv, core, x_lo, x_hi)
    weights = gather_weights(block)
    edges, inners = normalize(True, *norm_args), normalize(False, *norm_args)
    middle = edges + swap(*edges) + inners + swap(*inners)

    edge_near, inner_near = held_back((edges[0], inners[0]), block, *middle)
    beside = send(edge_near, swap_beside), send(inner_near, swap_beside)
    edge_far, inner_far = held_back((edges[1], inners[1]), weights)
    diagonal = send(edge_far, swap_diagonal), send(inner_far, swap_diagonal)

    def with_other(edge, inner):
        return (edge, *swap(edge), inner, *swap(inner))

    def exchange_rows(up, down):
        return send(down, next_row(1)), send(up, next_row(-1))

    key, value, up, down, query = project(True, place, *gains, weights, middle)
    *beside, up, down = project(
        False, place, *gains, weights, with_other(*beside), (up, down)
    )
    ends = exchange_rows(up, down)
    diagonal = held_back(diagonal, *beside)
    *diagonal, up, down = project(False, place, *gains, weights, with_other(*diagonal))
    ends += exchange_rows(up, down)
    arrays = (query, key, value, *beside, *diagonal)
    inner_away, inner_keep = attend(False, place, arrays)
    (inner_got,) = swap(inner_away)
    out = assemble(False, place, inner_keep, inner_got)
    edge_away, edge_keep = attend(True, place, arrays + ends)
    (edge_got,) = swap(edge_away)
    return assemble(True, place, edge_keep, edge_got, out)


def solution(mesh):
    in_specs = (
        P(None, "ha", "wa", None),
        P(None, "ha", "wa"),
        P(),
        P(),
        P(),
        P(),
        P(("ha", "wa"), None),
        P(),
        P(),
    )
    out_specs = P(None, "ha", "wa", None)
    return jax.shard_map(local, mesh=mesh, in_specs=in_specs, out_specs=out_specs, check_vma=False)
```
